32 devices in a mesh: rep: 2 (over y), lat: 8 (over z, x), blk: 2 (over core).
Axes of the slice: x: 2, y: 2, z: 4, core: 2. Of those that a mesh axis runs over, the one named last changes fastest.
Arguments:
- field: bfloat16 [32, 1440, 384], P(('rep', 'lat'), None, 'blk'), parts along dimension 0, may hold values from -6 to 6
- cotangent: bfloat16 [32, 1440, 384], P(('rep', 'lat'), None, 'blk'), parts along dimension 0, may hold values from -6 to 6
- first_weight: bfloat16 [4, 96, 192], replicated, may hold values from -0.4375 to 0.4375
- first_bias: float32 [4, 192], replicated, may hold values from -3 to 3
- second_weight: bfloat16 [4, 96, 192], replicated, may hold values from -0.4375 to 0.4375
- second_bias: float32 [4, 192], replicated, may hold values from -3 to 3
Outputs:
- mixed_field: bfloat16 [32, 1440, 384], P(('rep', 'lat'), None, 'blk'), parts along dimension 0
- field_gradient: bfloat16 [32, 1440, 384], P(('rep', 'lat'), None, 'blk'), parts along dimension 0
- first_gradient: float32 [8, 18432], P(('rep', 'blk'), 'lat'), parts along dimension 0
- second_gradient: float32 [8, 18432], P(('rep', 'blk'), 'lat'), parts along dimension 0
The draws below stay inside these ranges and needn't reach their ends.
There are 2 independent parts, one for each index of `rep`. The reference program is written for one: setup_inputs(seed, part) draws one part's arguments, and reference() takes and returns one part's arrays. A program takes and returns all parts, laid end to end along the dimension named above; an argument that names none is the same for every part. Nothing has to cross between parts.
All inputs are finite; a program needn't handle non-finite values.
Results may differ from the reference program's by a relative error of at most 0.0075.
The reference program's roundings to bfloat16 on the way count: a program that leaves them out, or rounds other values in their place, can miss the bound.
Values may be sent and summed in bfloat16 or wider, within the bound.
No kernel may reach another device: no remote copies, remote signals or barrier semaphores. Data moves between devices by JAX's collectives and lax.ppermute only.
A program may use at most 128 MiB of HBM per device.

```python
import math
import jax
import jax.numpy as jnp
from jax import lax

W = 1440
C = 384
CB = 96
KW = 512
G = 4
H = 16


def steps_of(own_key, dims, cuts, smallest, largest):
    level, own = 1.0, jax.random.fold_in(own_key, 6)
    for axis_at, shards_of in cuts:
        steps = jnp.exp(jax.random.uniform(jax.random.fold_in(own, axis_at), (shards_of,), jnp.float32, smallest / len(cuts), largest / len(cuts)))
        level = level * jnp.repeat(steps, dims[axis_at] // shards_of).reshape([-1 if axis == axis_at else 1 for axis in range(len(dims))])
    return level


def gaussian(own_key, shape, deviation, limit, split=(), kind=jnp.bfloat16):
    result = deviation * jax.random.normal(own_key, shape, jnp.float32)
    if split:
        result = result * steps_of(own_key, shape, split, -0.22, 0.18)
    return jnp.clip(result, -limit, limit).astype(kind)


def setup_inputs(seed: int = 0, part: int = 0) -> dict:
    arg_keys = jax.random.split(jax.random.key(seed), 7)
    own_keys = jax.random.split(jax.random.fold_in(arg_keys[6], part), 7)
    return {
        "field": gaussian(own_keys[0], (H, W, C), 1.0, 6.0, ((0, 8), (2, 2))),
        "cotangent": gaussian(own_keys[1], (H, W, C), 1.0, 6.0, ((0, 8), (2, 2))),
        "first_weight": gaussian(arg_keys[2], (G, CB, 2 * CB), (2 * CB) ** -0.5, 0.4375),
        "first_bias": gaussian(arg_keys[3], (G, 2 * CB), 0.5, 3.0, (), jnp.float32),
        "second_weight": gaussian(arg_keys[4], (G, CB, 2 * CB), (2 * CB) ** -0.5, 0.4375),
        "second_bias": gaussian(arg_keys[5], (G, 2 * CB), 0.5, 3.0, (), jnp.float32),
    }


SHRINK = 0.01
GELU_SCALE = 0.7978845608028654
GELU_CUBIC = 0.044715

def gelu_value(values):
    tangent = jnp.tanh(GELU_SCALE * (values + GELU_CUBIC * values * values * values))
    return 0.5 * values * (1.0 + tangent)

def gelu_slope(values):
    tangent = jnp.tanh(GELU_SCALE * (values + GELU_CUBIC * values * values * values))
    inner = GELU_SCALE * (1.0 + 3.0 * GELU_CUBIC * values * values)
    return 0.5 * (1.0 + tangent) + 0.5 * values * (1.0 - tangent * tangent) * inner

def zonal_tables(col_count, kept):
    column = jnp.arange(col_count, dtype=jnp.int32)
    wavenumber = jnp.arange(kept, dtype=jnp.int32)
    phases = column[:, None] * wavenumber[None, :] % col_count
    angles = phases.astype(jnp.float32) * (2.0 * math.pi / col_count)
    scaling = 1.0 / math.sqrt(col_count)
    cosine = jnp.cos(angles) * scaling
    sines = jnp.sin(angles) * scaling
    forward = jnp.stack([cosine, -sines], axis=1)
    factor = jnp.where(wavenumber == 0, 1.0, 2.0).astype(jnp.float32)[:, None]
    inverse = jnp.stack([cosine.T * factor, -sines.T * factor], axis=0)
    return (forward.astype(jnp.bfloat16), inverse.astype(jnp.bfloat16))

def meridian_tables(row_count):
    indices = jnp.arange(row_count, dtype=jnp.int32)
    phases = indices[:, None] * indices[None, :] % row_count
    angles = phases.astype(jnp.float32) * (2.0 * math.pi / row_count)
    scaling = 1.0 / math.sqrt(row_count)
    cosine = jnp.cos(angles) * scaling
    sines = jnp.sin(angles) * scaling
    forward = jnp.stack([jnp.stack([cosine, sines], axis=-1), jnp.stack([-sines, cosine], axis=-1)], axis=1)
    inverse = jnp.stack([jnp.stack([cosine, -sines], axis=-1), jnp.stack([sines, cosine], axis=-1)], axis=1)
    return (forward.astype(jnp.bfloat16), inverse.astype(jnp.bfloat16))

def contract(pattern, former, latter):
    return jnp.einsum(pattern, former.astype(jnp.float32), latter.astype(jnp.float32), precision=lax.Precision.HIGHEST)

def complex_block(weights):
    group_width = weights.shape[1]
    real_part = weights[:, :, :group_width]
    imag_part = weights[:, :, group_width:]
    upper = jnp.stack([real_part, imag_part], axis=2)
    lower = jnp.stack([-imag_part, real_part], axis=2)
    return jnp.stack([upper, lower], axis=1)

def block_gradient(outer):
    real_part = outer[:, 0, :, 0, :] + outer[:, 1, :, 1, :]
    imag_part = outer[:, 0, :, 1, :] - outer[:, 1, :, 0, :]
    return jnp.concatenate([real_part, imag_part], axis=2)

def bias_layout(bias):
    group_count = bias.shape[0]
    group_width = bias.shape[1] // 2
    return bias.reshape(group_count, 2, group_width).transpose(1, 0, 2)[None, :, None]

def spectral_forward(harmonics, first_block, second_block, first_shift, second_shift):
    row_count, _, wave_count, channels = harmonics.shape
    group_count = first_block.shape[0]
    group_width = first_block.shape[2]
    inputs = harmonics.reshape(row_count, 2, wave_count, group_count, group_width)
    pre_first = contract('mrkgc,grcsd->mskgd', inputs, first_block) + first_shift
    hidden = gelu_value(pre_first).astype(jnp.bfloat16)
    pre_second = contract('mrkgc,grcsd->mskgd', hidden, second_block) + second_shift
    shrunk = (pre_second - SHRINK * jnp.tanh(pre_second / SHRINK)).astype(jnp.bfloat16)
    return (inputs, pre_first, hidden, pre_second, shrunk.reshape(row_count, 2, wave_count, channels))

def spectral_backward(inputs, pre_first, hidden, pre_second, harmonic_adjoint, first_block, second_block):
    block_shape = pre_second.shape
    squashed = jnp.tanh(pre_second / SHRINK)
    second_adjoint = (harmonic_adjoint.reshape(block_shape) * (squashed * squashed)).astype(jnp.bfloat16)
    second_grad = block_gradient(contract('mrkgc,mskgd->grcsd', hidden, second_adjoint))
    hidden_adjoint = contract('mskgd,grcsd->mrkgc', second_adjoint, second_block)
    first_adjoint = (hidden_adjoint * gelu_slope(pre_first)).astype(jnp.bfloat16)
    first_grad = block_gradient(contract('mrkgc,mskgd->grcsd', inputs, first_adjoint))
    harmonics_adjoint = contract('mskgd,grcsd->mrkgc', first_adjoint, first_block).astype(jnp.bfloat16)
    row_count, _, wave_count, group_count, group_width = block_shape
    return (harmonics_adjoint.reshape(row_count, 2, wave_count, group_count * group_width), first_grad, second_grad)

def reference(field, cotangent, first_weight, first_bias, second_weight, second_bias):
    row_count, col_count, channels = field.shape
    group_count, group_width = (first_weight.shape[0], first_weight.shape[1])
    zonal_forward, zonal_inverse = zonal_tables(col_count, KW)
    meridian_forward, meridian_inverse = meridian_tables(row_count)
    field_groups = field.reshape(row_count, col_count, group_count, group_width).transpose(2, 0, 1, 3)
    cotangent_groups = cotangent.reshape(row_count, col_count, group_count, group_width).transpose(2, 0, 1, 3)

    def one_group(members):
        field_part, cotangent_part, weight_first, shift_first, weight_second, shift_second = members
        first_block = complex_block(weight_first[None])
        second_block = complex_block(weight_second[None])
        spectrum = contract('hwc,wrk->hrkc', field_part, zonal_forward).astype(jnp.bfloat16)
        adjoint = contract('hwc,rkw->hrkc', cotangent_part, zonal_inverse).astype(jnp.bfloat16)
        harmonics = contract('mphr,hrkc->mpkc', meridian_forward, spectrum).astype(jnp.bfloat16)
        harmonic_adjoint = contract('hrmp,hrkc->mpkc', meridian_inverse, adjoint)
        inputs, pre_first, hidden, pre_second, shrunk = spectral_forward(harmonics, first_block, second_block, bias_layout(shift_first[None]), bias_layout(shift_second[None]))
        harmonics_adjoint, first_grad, second_grad = spectral_backward(inputs, pre_first, hidden, pre_second, harmonic_adjoint, first_block, second_block)
        synthesis = contract('hrmp,mpkc->hrkc', meridian_inverse, shrunk).astype(jnp.bfloat16)
        harmonic_return = contract('mphr,mpkc->hrkc', meridian_forward, harmonics_adjoint).astype(jnp.bfloat16)
        mixed_part = (field_part.astype(jnp.float32) + contract('hrkc,rkw->hwc', synthesis, zonal_inverse)).astype(jnp.bfloat16)
        gradient_part = (cotangent_part.astype(jnp.float32) + contract('hrkc,wrk->hwc', harmonic_return, zonal_forward)).astype(jnp.bfloat16)
        return (mixed_part, gradient_part, first_grad[0], second_grad[0])
    mixed_parts, gradient_parts, first_grads, second_grads = lax.map(one_group, (field_groups, cotangent_groups, first_weight, first_bias, second_weight, second_bias))
    normalizer = 1.0 / math.sqrt(row_count * KW)
    mixed_field = mixed_parts.transpose(1, 2, 0, 3).reshape(row_count, col_count, channels)
    field_gradient = gradient_parts.transpose(1, 2, 0, 3).reshape(row_count, col_count, channels)
    first_gradient = (first_grads * normalizer).reshape(group_count, -1)
    second_gradient = (second_grads * normalizer).reshape(group_count, -1)
    return (mixed_field, field_gradient, first_gradient, second_gradient)
```

```python
import functools
import math

import jax
import jax.numpy as jnp
import numpy as np
from jax import lax
from jax.experimental import pallas as pl
from jax.experimental.pallas import tpu as pltpu
from jax.sharding import PartitionSpec as P

KW = 512
LANES = 128
HALF = 64
PACK = 16
VMEM_BYTES = 48 * 1024 * 1024

SHRINK = 0.01
GELU_SCALE = 0.7978845608028654
GELU_CUBIC = 0.044715
F32 = jnp.float32
BF16 = jnp.bfloat16


def zonal_waves(col_count, kept):
    column = np.arange(col_count, dtype=np.int64)
    wavenumber = np.arange(kept, dtype=np.int64)
    phases = column[:, None] * wavenumber[None, :] % col_count
    angles = phases.astype(np.float32) * np.float32(2.0 * math.pi / col_count)
    scaling = np.float32(1.0 / math.sqrt(col_count))
    cosine = np.cos(angles) * scaling
    sines = np.sin(angles) * scaling
    return np.stack([cosine, -sines], axis=1).astype(BF16)


def meridian_waves(row_count):
    indices = np.arange(row_count, dtype=np.int64)
    phases = indices[:, None] * indices[None, :] % row_count
    angles = phases.astype(np.float32) * np.float32(2.0 * math.pi / row_count)
    scaling = np.float32(1.0 / math.sqrt(row_count))
    return ((np.cos(angles) * scaling).astype(BF16), (np.sin(angles) * scaling).astype(BF16))


def wave_factor(kept):
    return np.where(np.arange(kept) == 0, 1.0, 2.0).astype(np.float32)


def mm(former, latter):
    return jnp.dot(former, latter, preferred_element_type=F32)


def swap_parts(values, first_sign):
    lane = lax.broadcasted_iota(jnp.int32, (1, LANES), 1)
    sign = jnp.where(lane < HALF, first_sign, -first_sign).astype(F32)
    return pltpu.roll(values, HALF, axis=1) * sign


def zonal_kernel(field_ref, table_ref, scale_ref, out_ref):
    result = (mm(field_ref[...], table_ref[...]) * scale_ref[...]).astype(BF16)
    for piece in range(out_ref.shape[0]):
        out_ref[piece] = result[:, piece * LANES : (piece + 1) * LANES]


def zonal(field_rows, table, scale, pieces):
    rows, col_count = field_rows.shape
    step = 2
    return pl.pallas_call(
        zonal_kernel,
        grid=(pieces // step,),
        in_specs=[
            pl.BlockSpec((rows, col_count), lambda i: (0, 0)),
            pl.BlockSpec((col_count, step * LANES), lambda i: (0, i)),
            pl.BlockSpec((1, step * LANES), lambda i: (0, i)),
        ],
        out_specs=pl.BlockSpec((step, rows, LANES), lambda i: (i, 0, 0)),
        out_shape=jax.ShapeDtypeStruct((pieces, rows, LANES), BF16),
        compiler_params=pltpu.CompilerParams(vmem_limit_bytes=VMEM_BYTES),
        cost_estimate=pl.CostEstimate(
            flops=2 * rows * col_count * pieces * LANES,
            bytes_accessed=2 * (rows * col_count + (col_count + rows) * pieces * LANES),
            transcendentals=0,
        ),
    )(field_rows, table, scale)


def inverse_kernel(scaled, modes_ref, table_ref, scale_ref, base_ref, out_ref):
    pieces = modes_ref.shape[0]
    modes = jnp.concatenate([modes_ref[piece] for piece in range(pieces)], axis=1)
    if scaled:
        modes = (modes.astype(F32) * scale_ref[...]).astype(BF16)
    out_ref[...] = (base_ref[...].astype(F32) + mm(modes, table_ref[...])).astype(BF16)


def inverse(modes, table, scale, base, scaled):
    pieces, rows, _ = modes.shape
    kept, col_count = table.shape
    width = 512
    return pl.pallas_call(
        functools.partial(inverse_kernel, scaled),
        grid=(pl.cdiv(col_count, width),),
        in_specs=[
            pl.BlockSpec((pieces, rows, LANES), lambda i: (0, 0, 0)),
            pl.BlockSpec((kept, width), lambda i: (0, i)),
            pl.BlockSpec((1, kept), lambda i: (0, 0)),
            pl.BlockSpec((rows, width), lambda i: (0, i)),
        ],
        out_specs=pl.BlockSpec((rows, width), lambda i: (0, i)),
        out_shape=jax.ShapeDtypeStruct((rows, col_count), BF16),
        compiler_params=pltpu.CompilerParams(vmem_limit_bytes=VMEM_BYTES),
        cost_estimate=pl.CostEstimate(
            flops=2 * rows * col_count * kept,
            bytes_accessed=2 * (2 * rows * col_count + (col_count + rows) * kept),
            transcendentals=0,
        ),
    )(modes, table, scale, base)


def meridian(load, mixer, first_sign, channels, store):
    count = mixer.shape[1] // PACK
    for start in range(0, channels, 2 * PACK):
        pair = jnp.concatenate(
            [load(start + shift).reshape(count * PACK, LANES) for shift in (0, PACK)], axis=1
        )
        both = mm(mixer[...], pair)
        for index in range(2):
            half = both[:, index * LANES : (index + 1) * LANES]
            value = half[: count * PACK] + swap_parts(half[count * PACK :], first_sign)
            store(start + index * PACK, value.reshape(count, PACK, LANES))


def complex_dot(weights, operand, first_sign):
    width = weights.shape[0] // 2
    both = mm(weights, jnp.concatenate(operand, axis=1))
    return [
        both[:width, i * LANES : (i + 1) * LANES]
        + swap_parts(both[width:, i * LANES : (i + 1) * LANES], first_sign)
        for i in range(len(operand))
    ]


def forward_kernel(
    modes_ref, mixer_ref, first_ref, first_bias_ref, second_ref, second_bias_ref,
    out_ref, harm_ref, hidden_ref, slope_ref, gate_ref, shrunk_ref,
):
    count, channels, _ = modes_ref.shape
    groups, _, width = first_ref.shape

    def keep(start, value):
        harm_ref[:, start : start + PACK, :] = value.astype(BF16)

    meridian(lambda c: modes_ref[:, c : c + PACK, :], mixer_ref, 1.0, channels, keep)
    for group in range(groups):
        span = slice(group * width, (group + 1) * width)
        for row in range(0, count, 2):
            pre = complex_dot(first_ref[group], [harm_ref[row + i, span, :] for i in range(2)], -1.0)
            hidden = []
            for i in range(2):
                v = pre[i] + first_bias_ref[group]
                square = v * v
                tangent = jnp.tanh(GELU_SCALE * (v + GELU_CUBIC * square * v))
                outer = 0.5 * (1.0 + tangent)
                inner = GELU_SCALE * (1.0 + 3.0 * GELU_CUBIC * square)
                hidden.append((v * outer).astype(BF16))
                hidden_ref[row + i, span, :] = hidden[i]
                slope_ref[row + i, span, :] = outer + 0.5 * v * (1.0 - tangent * tangent) * inner
            pre = complex_dot(second_ref[group], hidden, -1.0)
            for i in range(2):
                v = pre[i] + second_bias_ref[group]
                squashed = jnp.tanh(v * (1.0 / SHRINK))
                shrunk_ref[row + i, span, :] = (v - SHRINK * squashed).astype(BF16)
                gate_ref[row + i, span, :] = squashed * squashed

    def emit(start, value):
        out_ref[:, start : start + PACK, :] = value.astype(BF16)

    meridian(lambda c: shrunk_ref[:, c : c + PACK, :], mixer_ref, -1.0, channels, emit)


def whole(*shape):
    return pl.BlockSpec(shape, lambda: (0,) * len(shape))


def forward_middle(modes, mixer, first, first_bias, second, second_bias):
    shape = modes.shape
    size = math.prod(shape)
    kinds = (BF16, BF16, BF16, F32, F32)
    return pl.pallas_call(
        forward_kernel,
        in_specs=[whole(*a.shape) for a in (modes, mixer, first, first_bias, second, second_bias)],
        out_specs=[whole(*shape) for _ in kinds],
        out_shape=[jax.ShapeDtypeStruct(shape, kind) for kind in kinds],
        scratch_shapes=[pltpu.VMEM(shape, BF16)],
        compiler_params=pltpu.CompilerParams(vmem_limit_bytes=VMEM_BYTES),
        cost_estimate=pl.CostEstimate(
            flops=4 * size * 1024, bytes_accessed=16 * size, transcendentals=2 * size
        ),
    )(modes, mixer, first, first_bias, second, second_bias)


def nt(former, latter):
    return lax.dot_general(former, latter, (((1,), (1,)), ((), ())), preferred_element_type=F32)


def backward_kernel(
    normalizer, modes_ref, mixer_ref, first_ref, second_ref, harm_ref, hidden_ref, slope_ref, gate_ref,
    out_ref, grad_ref, adjoint_ref, back_ref,
):
    count, channels, _ = modes_ref.shape
    groups, _, width = first_ref.shape

    def keep(start, value):
        adjoint_ref[:, start : start + PACK, :] = value * gate_ref[:, start : start + PACK, :]

    meridian(lambda c: modes_ref[:, c : c + PACK, :], mixer_ref, 1.0, channels, keep)
    for group in range(groups):
        span = slice(group * width, (group + 1) * width)
        first_sum = jnp.zeros((width, 2 * width), F32)
        second_sum = jnp.zeros((width, 2 * width), F32)
        for row in range(0, count, 2):
            exact = [adjoint_ref[row + i, span, :] for i in range(2)]
            second_adjoint = [a.astype(BF16) for a in exact]
            turned = [swap_parts(a, 1.0).astype(BF16) for a in exact]
            stacked = jnp.concatenate(
                [jnp.concatenate(second_adjoint, axis=1), jnp.concatenate(turned, axis=1)], axis=0
            )
            hidden = jnp.concatenate([hidden_ref[row + i, span, :] for i in range(2)], axis=1)
            second_sum += nt(hidden, stacked)
            back = complex_dot(second_ref[group], second_adjoint, 1.0)
            exact = [back[i] * slope_ref[row + i, span, :] for i in range(2)]
            first_adjoint = [a.astype(BF16) for a in exact]
            turned = [swap_parts(a, 1.0).astype(BF16) for a in exact]
            stacked = jnp.concatenate(
                [jnp.concatenate(first_adjoint, axis=1), jnp.concatenate(turned, axis=1)], axis=0
            )
            inputs = jnp.concatenate([harm_ref[row + i, span, :] for i in range(2)], axis=1)
            first_sum += nt(inputs, stacked)
            back = complex_dot(first_ref[group], first_adjoint, 1.0)
            for i in range(2):
                back_ref[row + i, span, :] = back[i].astype(BF16)
        grad_ref[0, group] = first_sum * normalizer
        grad_ref[1, group] = second_sum * normalizer

    def emit(start, value):
        out_ref[:, start : start + PACK, :] = value.astype(BF16)

    meridian(lambda c: back_ref[:, c : c + PACK, :], mixer_ref, -1.0, channels, emit)


def backward_middle(modes, mixer, first, second, harm, hidden, slope, gate, normalizer):
    shape = modes.shape
    size = math.prod(shape)
    groups, twice, width = first.shape
    operands = (modes, mixer, first, second, harm, hidden, slope, gate)
    grad_shape = (2, groups, width, twice)
    return pl.pallas_call(
        functools.partial(backward_kernel, normalizer),
        in_specs=[whole(*a.shape) for a in operands],
        out_specs=[whole(*shape), whole(*grad_shape)],
        out_shape=[jax.ShapeDtypeStruct(shape, BF16), jax.ShapeDtypeStruct(grad_shape, F32)],
        scratch_shapes=[pltpu.VMEM(shape, F32), pltpu.VMEM(shape, BF16)],
        compiler_params=pltpu.CompilerParams(vmem_limit_bytes=VMEM_BYTES),
        cost_estimate=pl.CostEstimate(
            flops=4 * size * 1024, bytes_accessed=16 * size, transcendentals=0
        ),
    )(*operands)


def local_groups_of(array, groups):
    return lax.dynamic_slice_in_dim(array, lax.axis_index("blk") * groups, groups, axis=0)


def exchange(blocks):
    return lax.all_to_all(blocks, "lat", split_axis=0, concat_axis=0, tiled=True)


def reduce_gradients(grads, lat_count):
    kinds, groups, width, twice = grads.shape
    piece = width * twice // lat_count
    split = grads.reshape(kinds * groups, lat_count, piece).transpose(1, 0, 2)
    if kinds * groups * piece % LANES == 0:
        split = split.reshape(lat_count, kinds * groups * piece // LANES, LANES)
    total = jnp.sum(exchange(split), axis=0)
    return total.reshape(kinds, groups, piece)


def with_kernels(field, cotangent, first_weight, first_bias, second_weight, second_bias):
    local_rows, col_count, channels = field.shape
    width = first_weight.shape[1]
    groups = channels // width
    lat_count = lax.axis_size("lat")
    row_count = local_rows * lat_count
    sub_count = KW // lat_count
    waves = zonal_waves(col_count, KW)
    table = (
        waves.reshape(col_count, 2, lat_count, sub_count).transpose(0, 2, 1, 3).reshape(col_count, 2 * KW)
    )
    factor = np.repeat(wave_factor(KW).reshape(lat_count, 1, sub_count), 2, axis=1).reshape(1, 2 * KW)
    cosine, sines = meridian_waves(row_count)
    unit = np.eye(PACK, dtype=np.float32)
    mixer = np.concatenate(
        [np.kron(cosine.astype(np.float32), unit), np.kron(sines.astype(np.float32), unit)], axis=0
    ).astype(BF16)
    ahead, back = jnp.asarray(table), jnp.asarray(np.ascontiguousarray(table.T))
    factor, ones = jnp.asarray(factor), jnp.ones((1, 2 * KW), F32)
    mixer = jnp.asarray(mixer)

    def rows_of(array):
        return array.transpose(0, 2, 1).reshape(local_rows * channels, col_count)

    def grid_of(rows):
        return rows.reshape(local_rows, channels, col_count).transpose(0, 2, 1)

    def spread(blocks):
        return exchange(blocks).reshape(row_count, channels, LANES)

    def gather(modes):
        return exchange(modes.reshape(lat_count, local_rows * channels, LANES))

    def bias_lanes(bias):
        parts = local_groups_of(bias, groups).reshape(groups, 2, width, 1)
        wide = jnp.broadcast_to(parts, (groups, 2, width, sub_count))
        return wide.transpose(0, 2, 1, 3).reshape(groups, width, LANES)

    def tall(weight):
        return jnp.concatenate([weight[:, :, :width], weight[:, :, width:]], axis=1)

    own_first = local_groups_of(first_weight, groups)
    own_second = local_groups_of(second_weight, groups)
    field_rows, cotangent_rows = rows_of(field), rows_of(cotangent)
    modes = spread(zonal(field_rows, ahead, ones, lat_count))
    adjoint = spread(zonal(cotangent_rows, ahead, factor, lat_count))
    synthesis, harm, hidden, slope, gate = forward_middle(
        modes, mixer,
        own_first.transpose(0, 2, 1), bias_lanes(first_bias),
        own_second.transpose(0, 2, 1), bias_lanes(second_bias),
    )
    mixed_modes = gather(synthesis)
    returned, grads = backward_middle(
        adjoint, mixer, tall(own_first), tall(own_second), harm, hidden, slope, gate,
        1.0 / math.sqrt(row_count * KW),
    )
    return_modes = gather(returned)
    gradients = reduce_gradients(grads, lat_count)
    mixed = inverse(mixed_modes, back, factor, field_rows, True)
    field_gradient = inverse(return_modes, back, factor, cotangent_rows, False)
    return (grid_of(mixed), grid_of(field_gradient), gradients[0], gradients[1])


def gelu_value(values):
    tangent = jnp.tanh(GELU_SCALE * (values + GELU_CUBIC * values * values * values))
    return 0.5 * values * (1.0 + tangent)


def gelu_slope(values):
    tangent = jnp.tanh(GELU_SCALE * (values + GELU_CUBIC * values * values * values))
    inner = GELU_SCALE * (1.0 + 3.0 * GELU_CUBIC * values * values)
    return 0.5 * (1.0 + tangent) + 0.5 * values * (1.0 - tangent * tangent) * inner


def contract(pattern, former, latter):
    return jnp.einsum(pattern, former, latter, preferred_element_type=F32)


def complex_block(weights):
    width = weights.shape[1]
    real_part, imag_part = weights[:, :, :width], weights[:, :, width:]
    upper = jnp.stack([real_part, imag_part], axis=2)
    lower = jnp.stack([-imag_part, real_part], axis=2)
    return jnp.stack([upper, lower], axis=1)


def block_gradient(outer):
    real_part = outer[:, 0, :, 0, :] + outer[:, 1, :, 1, :]
    imag_part = outer[:, 0, :, 1, :] - outer[:, 1, :, 0, :]
    return jnp.concatenate([real_part, imag_part], axis=2)


def bias_layout(bias):
    groups, twice = bias.shape
    return bias.reshape(groups, 2, twice // 2).transpose(1, 0, 2)[None, :, None]


def plain(field, cotangent, first_weight, first_bias, second_weight, second_bias):
    local_rows, col_count, channels = field.shape
    width = first_weight.shape[1]
    groups = channels // width
    lat_count = lax.axis_size("lat")
    row_count = local_rows * lat_count
    ahead = jnp.asarray(zonal_waves(col_count, KW))
    factor = jnp.asarray(wave_factor(KW))
    cosine, sines = (jnp.asarray(t) for t in meridian_waves(row_count))
    forth = jnp.stack(
        [jnp.stack([cosine, sines], axis=-1), jnp.stack([-sines, cosine], axis=-1)], axis=1
    )
    first_block = complex_block(local_groups_of(first_weight, groups))
    second_block = complex_block(local_groups_of(second_weight, groups))

    def swap(array, split, concat):
        return lax.all_to_all(array, "lat", split_axis=split, concat_axis=concat, tiled=True)

    spectrum = contract("hwc,wrk->hrkc", field, ahead).astype(BF16)
    adjoint = (contract("hwc,wrk->hrkc", cotangent, ahead) * factor[:, None]).astype(BF16)
    modes, adjoint = swap(spectrum, 2, 0), swap(adjoint, 2, 0)
    block_shape = (row_count, 2, modes.shape[2], groups, width)
    inputs = contract("mphr,hrkc->mpkc", forth, modes).astype(BF16).reshape(block_shape)
    harmonic_adjoint = contract("mphr,hrkc->mpkc", forth, adjoint).reshape(block_shape)
    pre_first = contract("mrkgc,grcsd->mskgd", inputs, first_block) + bias_layout(
        local_groups_of(first_bias, groups)
    )
    hidden = gelu_value(pre_first).astype(BF16)
    pre_second = contract("mrkgc,grcsd->mskgd", hidden, second_block) + bias_layout(
        local_groups_of(second_bias, groups)
    )
    squashed = jnp.tanh(pre_second / SHRINK)
    shrunk = (pre_second - SHRINK * squashed).astype(BF16).reshape(modes.shape)
    second_adjoint = (harmonic_adjoint * (squashed * squashed)).astype(BF16)
    second_grad = block_gradient(contract("mrkgc,mskgd->grcsd", hidden, second_adjoint))
    hidden_adjoint = contract("mskgd,grcsd->mrkgc", second_adjoint, second_block)
    first_adjoint = (hidden_adjoint * gelu_slope(pre_first)).astype(BF16)
    first_grad = block_gradient(contract("mrkgc,mskgd->grcsd", inputs, first_adjoint))
    harmonics_adjoint = contract("mskgd,grcsd->mrkgc", first_adjoint, first_block).astype(BF16)
    synthesis = contract("mphr,mpkc->hrkc", forth, shrunk).astype(BF16)
    returned = contract(
        "mphr,mpkc->hrkc", forth, harmonics_adjoint.reshape(modes.shape)
    ).astype(BF16)
    mixed_modes, return_modes = swap(synthesis, 0, 2), swap(returned, 0, 2)
    gradients = reduce_gradients(
        jnp.stack([first_grad, second_grad]) * (1.0 / math.sqrt(row_count * KW)), lat_count
    )
    mixed_modes = (mixed_modes.astype(F32) * factor[:, None]).astype(BF16)
    mixed = (field.astype(F32) + contract("hrkc,wrk->hwc", mixed_modes, ahead)).astype(BF16)
    field_gradient = (
        cotangent.astype(F32) + contract("hrkc,wrk->hwc", return_modes, ahead)
    ).astype(BF16)
    return (mixed, field_gradient, gradients[0], gradients[1])


def on_device(field, *rest):
    local_rows, _, channels = field.shape
    lat_count = lax.axis_size("lat")
    fits = (
        KW == HALF * lat_count
        and channels % (2 * PACK) == 0
        and local_rows * lat_count % 2 == 0
        and rest[1].shape[1] % PACK == 0
        and local_rows * lat_count * PACK <= 512
    )
    return (with_kernels if fits else plain)(field, *rest)


def solution(mesh):
    placed = (P(("rep", "lat"), None, "blk"), P(("rep", "lat"), None, "blk"), P(), P(), P(), P())
    return jax.shard_map(
        on_device,
        mesh=mesh,
        in_specs=placed,
        out_specs=(
            P(("rep", "lat"), None, "blk"),
            P(("rep", "lat"), None, "blk"),
            P(("rep", "blk"), "lat"),
            P(("rep", "blk"), "lat"),
        ),
        check_vma=False,
    )
```

```python
import functools
import math

import jax
import jax.numpy as jnp
import numpy as np
from jax import lax
from jax.experimental import pallas as pl
from jax.experimental.pallas import tpu as pltpu
from jax.sharding import PartitionSpec as P

KW = 512
LANES = 128
HALF = 64
PACK = 16
VMEM_BYTES = 60 * 1024 * 1024

SHRINK = 0.01
GELU_SCALE = 0.7978845608028654
GELU_CUBIC = 0.044715
F32 = jnp.float32
BF16 = jnp.bfloat16


def zonal_waves(col_count, kept):
    column = np.arange(col_count, dtype=np.int64)
    wavenumber = np.arange(kept, dtype=np.int64)
    phases = column[:, None] * wavenumber[None, :] % col_count
    angles = phases.astype(np.float32) * np.float32(2.0 * math.pi / col_count)
    scaling = np.float32(1.0 / math.sqrt(col_count))
    cosine = np.cos(angles) * scaling
    sines = np.sin(angles) * scaling
    return np.stack([cosine, -sines], axis=1).astype(BF16)


def meridian_waves(row_count):
    indices = np.arange(row_count, dtype=np.int64)
    phases = indices[:, None] * indices[None, :] % row_count
    angles = phases.astype(np.float32) * np.float32(2.0 * math.pi / row_count)
    scaling = np.float32(1.0 / math.sqrt(row_count))
    return ((np.cos(angles) * scaling).astype(BF16), (np.sin(angles) * scaling).astype(BF16))


def wave_factor(kept):
    return np.where(np.arange(kept) == 0, 1.0, 2.0).astype(np.float32)


def mm(former, latter):
    return jnp.dot(former, latter, preferred_element_type=F32)


def swap_parts(values, first_sign):
    lane = lax.broadcasted_iota(jnp.int32, (1, LANES), 1)
    sign = jnp.where(lane < HALF, first_sign, -first_sign).astype(F32)
    return pltpu.roll(values, HALF, axis=1) * sign


def relative(mine, shift):
    return jnp.bitwise_xor(mine, shift)


def zonal_kernel(mine_ref, field_ref, table_ref, scale_ref, *rest):
    outs, pair_ref = rest[:-1], rest[-1]
    odd = jnp.bitwise_and(mine_ref[0], 1)
    result = (mm(field_ref[...], table_ref[...]) * scale_ref[...]).astype(BF16)
    for piece in range(2):
        pair_ref[piece] = result[:, piece * LANES : (piece + 1) * LANES]
    step = pl.program_id(0)
    for place in range(len(outs) // 2):

        @pl.when(step == place)
        def _():
            outs[2 * place][...] = pair_ref[odd]
            outs[2 * place + 1][...] = pair_ref[1 - odd]


def zonal(mine, field_rows, table, scale, pieces):
    rows, col_count = field_rows.shape
    wide = 2 * LANES

    def block_of(i, place):
        return (0, jnp.bitwise_xor(lax.shift_right_logical(place[0], 1), i))

    return pl.pallas_call(
        zonal_kernel,
        grid_spec=pltpu.PrefetchScalarGridSpec(
            num_scalar_prefetch=1,
            grid=(pieces // 2,),
            in_specs=[
                pl.BlockSpec((rows, col_count), lambda i, place: (0, 0)),
                pl.BlockSpec((col_count, wide), block_of),
                pl.BlockSpec((1, wide), block_of),
            ],
            out_specs=[pl.BlockSpec((rows, LANES), lambda i, place: (0, 0)) for _ in range(pieces)],
            scratch_shapes=[pltpu.VMEM((2, rows, LANES), BF16)],
        ),
        out_shape=[jax.ShapeDtypeStruct((rows, LANES), BF16) for _ in range(pieces)],
        compiler_params=pltpu.CompilerParams(vmem_limit_bytes=VMEM_BYTES),
        cost_estimate=pl.CostEstimate(
            flops=2 * rows * col_count * pieces * LANES,
            bytes_accessed=2 * (rows * col_count + (col_count + rows) * pieces * LANES),
            transcendentals=0,
        ),
    )(mine, field_rows, table, scale)


def inverse_kernel(scaled, pieces, *refs):
    blocks, (table_ref, scale_ref, base_ref, out_ref, modes_ref) = refs[:pieces], refs[pieces:]

    @pl.when(pl.program_id(0) == 0)
    def _():
        mine = lax.axis_index("lat")
        for shift in range(pieces):
            modes_ref[relative(mine, shift)] = blocks[shift][...]

    modes = jnp.concatenate([modes_ref[piece] for piece in range(pieces)], axis=1)
    if scaled:
        modes = (modes.astype(F32) * scale_ref[...]).astype(BF16)
    out_ref[...] = (base_ref[...].astype(F32) + mm(modes, table_ref[...])).astype(BF16)


def inverse(blocks, table, scale, base, scaled):
    pieces = len(blocks)
    rows, _ = blocks[0].shape
    kept, col_count = table.shape
    width = 512
    return pl.pallas_call(
        functools.partial(inverse_kernel, scaled, pieces),
        grid=(pl.cdiv(col_count, width),),
        in_specs=[pl.BlockSpec((rows, LANES), lambda i: (0, 0)) for _ in blocks]
        + [
            pl.BlockSpec((kept, width), lambda i: (0, i)),
            pl.BlockSpec((1, kept), lambda i: (0, 0)),
            pl.BlockSpec((rows, width), lambda i: (0, i)),
        ],
        out_specs=pl.BlockSpec((rows, width), lambda i: (0, i)),
        out_shape=jax.ShapeDtypeStruct((rows, col_count), BF16),
        scratch_shapes=[pltpu.VMEM((pieces, rows, LANES), BF16)],
        compiler_params=pltpu.CompilerParams(vmem_limit_bytes=VMEM_BYTES),
        cost_estimate=pl.CostEstimate(
            flops=2 * rows * col_count * kept,
            bytes_accessed=2 * (2 * rows * col_count + (col_count + rows) * kept),
            transcendentals=0,
        ),
    )(*blocks, table, scale, base)


def meridian(load, mixer, first_sign, channels, store):
    count = mixer.shape[1] // PACK
    for start in range(0, channels, 2 * PACK):
        pair = jnp.concatenate(
            [load(start + shift).reshape(count * PACK, LANES) for shift in (0, PACK)], axis=1
        )
        both = mm(mixer[...], pair)
        for index in range(2):
            half = both[:, index * LANES : (index + 1) * LANES]
            value = half[: count * PACK] + swap_parts(half[count * PACK :], first_sign)
            store(start + index * PACK, value.reshape(count, PACK, LANES))


def complex_dot(weights, operand, first_sign):
    width = weights.shape[0] // 2
    both = mm(weights, jnp.concatenate(operand, axis=1))
    return [
        both[:width, i * LANES : (i + 1) * LANES]
        + swap_parts(both[width:, i * LANES : (i + 1) * LANES], first_sign)
        for i in range(len(operand))
    ]


def collect(blocks, modes_ref):
    mine = lax.axis_index("lat")
    rows = modes_ref.shape[0] // len(blocks)
    for shift, block in enumerate(blocks):
        for row in range(rows):
            channels = modes_ref.shape[1]
            modes_ref[relative(mine, shift) * rows + row] = block[row * channels : (row + 1) * channels]


def distribute(modes_ref, outs):
    mine = lax.axis_index("lat")
    rows = modes_ref.shape[0] // len(outs)
    channels = modes_ref.shape[1]
    for shift, out in enumerate(outs):
        for row in range(rows):
            out[row * channels : (row + 1) * channels] = modes_ref[relative(mine, shift) * rows + row]


def forward_kernel(pieces, *refs):
    blocks, refs = refs[:pieces], refs[pieces:]
    (mixer_ref, first_ref, first_bias_ref, second_ref, second_bias_ref), refs = refs[:5], refs[5:]
    outs, refs = refs[:pieces], refs[pieces:]
    harm_ref, hidden_ref, slope_ref, gate_ref, modes_ref, shrunk_ref = refs
    collect(blocks, modes_ref)
    count, channels, _ = modes_ref.shape
    groups, _, width = first_ref.shape

    def keep(start, value):
        harm_ref[:, start : start + PACK, :] = value.astype(BF16)

    meridian(lambda c: modes_ref[:, c : c + PACK, :], mixer_ref, 1.0, channels, keep)
    for group in range(groups):
        span = slice(group * width, (group + 1) * width)
        for row in range(0, count, 2):
            pre = complex_dot(first_ref[group], [harm_ref[row + i, span, :] for i in range(2)], -1.0)
            hidden = []
            for i in range(2):
                v = pre[i] + first_bias_ref[group]
                square = v * v
                tangent = jnp.tanh(GELU_SCALE * (v + GELU_CUBIC * square * v))
                outer = 0.5 * (1.0 + tangent)
                inner = GELU_SCALE * (1.0 + 3.0 * GELU_CUBIC * square)
                hidden.append((v * outer).astype(BF16))
                hidden_ref[row + i, span, :] = hidden[i]
                slope_ref[row + i, span, :] = outer + 0.5 * v * (1.0 - tangent * tangent) * inner
            pre = complex_dot(second_ref[group], hidden, -1.0)
            for i in range(2):
                v = pre[i] + second_bias_ref[group]
                squashed = jnp.tanh(v * (1.0 / SHRINK))
                shrunk_ref[row + i, span, :] = (v - SHRINK * squashed).astype(BF16)
                gate_ref[row + i, span, :] = squashed * squashed

    def emit(start, value):
        modes_ref[:, start : start + PACK, :] = value.astype(BF16)

    meridian(lambda c: shrunk_ref[:, c : c + PACK, :], mixer_ref, -1.0, channels, emit)
    distribute(modes_ref, outs)


def whole(*shape):
    return pl.BlockSpec(shape, lambda: (0,) * len(shape))


def forward_middle(blocks, channels, mixer, first, first_bias, second, second_bias):
    pieces = len(blocks)
    shape = (pieces * blocks[0].shape[0] // channels, channels, LANES)
    size = math.prod(shape)
    kinds = (BF16, BF16, F32, F32)
    operands = (*blocks, mixer, first, first_bias, second, second_bias)
    results = pl.pallas_call(
        functools.partial(forward_kernel, pieces),
        in_specs=[whole(*a.shape) for a in operands],
        out_specs=[whole(*a.shape) for a in blocks] + [whole(*shape) for _ in kinds],
        out_shape=[jax.ShapeDtypeStruct(a.shape, BF16) for a in blocks]
        + [jax.ShapeDtypeStruct(shape, kind) for kind in kinds],
        scratch_shapes=[pltpu.VMEM(shape, BF16), pltpu.VMEM(shape, BF16)],
        compiler_params=pltpu.CompilerParams(vmem_limit_bytes=VMEM_BYTES),
        cost_estimate=pl.CostEstimate(
            flops=4 * size * 1024, bytes_accessed=16 * size, transcendentals=2 * size
        ),
    )(*operands)
    return results[:pieces], results[pieces:]


def nt(former, latter):
    return lax.dot_general(former, latter, (((1,), (1,)), ((), ())), preferred_element_type=F32)


def backward_kernel(normalizer, pieces, *refs):
    blocks, refs = refs[:pieces], refs[pieces:]
    mixer_ref, first_ref, second_ref, harm_ref, hidden_ref, slope_ref, gate_ref = refs[:7]
    outs, grad_ref = refs[7 : 7 + pieces], refs[7 + pieces]
    modes_ref, adjoint_ref, back_ref = refs[8 + pieces :]
    collect(blocks, modes_ref)
    mine = lax.axis_index("lat")
    count, channels, _ = modes_ref.shape
    groups, _, width = first_ref.shape

    def keep(start, value):
        adjoint_ref[:, start : start + PACK, :] = value * gate_ref[:, start : start + PACK, :]

    meridian(lambda c: modes_ref[:, c : c + PACK, :], mixer_ref, 1.0, channels, keep)
    for group in range(groups):
        span = slice(group * width, (group + 1) * width)
        first_sum = jnp.zeros((width, 2 * width), F32)
        second_sum = jnp.zeros((width, 2 * width), F32)
        for row in range(0, count, 2):
            exact = [adjoint_ref[row + i, span, :] for i in range(2)]
            second_adjoint = [a.astype(BF16) for a in exact]
            turned = [swap_parts(a, 1.0).astype(BF16) for a in exact]
            stacked = jnp.concatenate(
                [jnp.concatenate(second_adjoint, axis=1), jnp.concatenate(turned, axis=1)], axis=0
            )
            hidden = jnp.concatenate([hidden_ref[row + i, span, :] for i in range(2)], axis=1)
            second_sum += nt(hidden, stacked)
            back = complex_dot(second_ref[group], second_adjoint, 1.0)
            exact = [back[i] * slope_ref[row + i, span, :] for i in range(2)]
            first_adjoint = [a.astype(BF16) for a in exact]
            turned = [swap_parts(a, 1.0).astype(BF16) for a in exact]
            stacked = jnp.concatenate(
                [jnp.concatenate(first_adjoint, axis=1), jnp.concatenate(turned, axis=1)], axis=0
            )
            inputs = jnp.concatenate([harm_ref[row + i, span, :] for i in range(2)], axis=1)
            first_sum += nt(inputs, stacked)
            back = complex_dot(first_ref[group], first_adjoint, 1.0)
            for i in range(2):
                back_ref[row + i, span, :] = back[i].astype(BF16)
        part = width // pieces
        for kind, total in enumerate((first_sum * normalizer, second_sum * normalizer)):
            begin = (kind * groups + group) * part
            for piece in range(pieces):
                grad_ref[relative(mine, piece), begin : begin + part, :] = total[
                    piece * part : (piece + 1) * part
                ]

    def emit(start, value):
        modes_ref[:, start : start + PACK, :] = value.astype(BF16)

    meridian(lambda c: back_ref[:, c : c + PACK, :], mixer_ref, -1.0, channels, emit)
    distribute(modes_ref, outs)


def backward_middle(blocks, channels, mixer, first, second, saved, normalizer):
    pieces = len(blocks)
    shape = (pieces * blocks[0].shape[0] // channels, channels, LANES)
    size = math.prod(shape)
    groups, twice, width = first.shape
    operands = (*blocks, mixer, first, second, *saved)
    grad_shape = (pieces, 2 * groups * width // pieces, twice)
    results = pl.pallas_call(
        functools.partial(backward_kernel, normalizer, pieces),
        in_specs=[whole(*a.shape) for a in operands],
        out_specs=[whole(*a.shape) for a in blocks] + [whole(*grad_shape)],
        out_shape=[jax.ShapeDtypeStruct(a.shape, BF16) for a in blocks]
        + [jax.ShapeDtypeStruct(grad_shape, F32)],
        scratch_shapes=[pltpu.VMEM(shape, BF16), pltpu.VMEM(shape, F32), pltpu.VMEM(shape, BF16)],
        compiler_params=pltpu.CompilerParams(vmem_limit_bytes=VMEM_BYTES),
        cost_estimate=pl.CostEstimate(
            flops=4 * size * 1024, bytes_accessed=16 * size, transcendentals=0
        ),
    )(*operands)
    return results[:pieces], results[pieces]


def local_groups_of(array, groups):
    return lax.dynamic_slice_in_dim(array, lax.axis_index("blk") * groups, groups, axis=0)


def exchange(blocks):
    return lax.all_to_all(blocks, "lat", split_axis=0, concat_axis=0, tiled=True)


def pass_to(block, shift):
    count = lax.axis_size("lat")
    return lax.ppermute(block, "lat", [(place, place ^ shift) for place in range(count)])


ORDER = (4, 5, 6, 7, 2, 3, 1)


def swap_blocks(blocks):
    result = list(blocks)
    for shift in sorted(range(1, len(blocks)), key=lambda s: ORDER.index(s) if s in ORDER else s):
        result[shift] = pass_to(blocks[shift], shift)
    return result


def halve_gradients(grads):
    count = grads.shape[0]
    bit = 1
    while bit < count:
        pairs = grads.reshape(-1, 2, *grads.shape[1:])
        grads = pairs[:, 0] + pass_to(pairs[:, 1], bit)
        bit *= 2
    return grads[0]


def reduce_gradients(grads, lat_count):
    kinds, groups, width, twice = grads.shape
    piece = width * twice // lat_count
    split = grads.reshape(kinds * groups, lat_count, piece).transpose(1, 0, 2)
    if kinds * groups * piece % LANES == 0:
        split = split.reshape(lat_count, kinds * groups * piece // LANES, LANES)
    total = jnp.sum(exchange(split), axis=0)
    return total.reshape(kinds, groups, piece)


def with_kernels(field, cotangent, first_weight, first_bias, second_weight, second_bias):
    local_rows, col_count, channels = field.shape
    width = first_weight.shape[1]
    groups = channels // width
    lat_count = lax.axis_size("lat")
    row_count = local_rows * lat_count
    sub_count = KW // lat_count
    waves = zonal_waves(col_count, KW)
    table = (
        waves.reshape(col_count, 2, lat_count, sub_count).transpose(0, 2, 1, 3).reshape(col_count, 2 * KW)
    )
    factor = np.repeat(wave_factor(KW).reshape(lat_count, 1, sub_count), 2, axis=1).reshape(1, 2 * KW)
    cosine, sines = meridian_waves(row_count)
    unit = np.eye(PACK, dtype=np.float32)
    mixer = np.concatenate(
        [np.kron(cosine.astype(np.float32), unit), np.kron(sines.astype(np.float32), unit)], axis=0
    ).astype(BF16)
    ahead, back = jnp.asarray(table), jnp.asarray(np.ascontiguousarray(table.T))
    factor, ones = jnp.asarray(factor), jnp.ones((1, 2 * KW), F32)
    mixer = jnp.asarray(mixer)

    def rows_of(array):
        return array.transpose(0, 2, 1).reshape(local_rows * channels, col_count)

    def grid_of(rows):
        return rows.reshape(local_rows, channels, col_count).transpose(0, 2, 1)

    def bias_lanes(bias):
        parts = local_groups_of(bias, groups).reshape(groups, 2, width, 1)
        wide = jnp.broadcast_to(parts, (groups, 2, width, sub_count))
        return wide.transpose(0, 2, 1, 3).reshape(groups, width, LANES)

    def tall(weight):
        return jnp.concatenate([weight[:, :, :width], weight[:, :, width:]], axis=1)

    own_first = local_groups_of(first_weight, groups)
    own_second = local_groups_of(second_weight, groups)
    field_rows, cotangent_rows = rows_of(field), rows_of(cotangent)
    mine = lax.axis_index("lat").astype(jnp.int32).reshape(1)
    modes = swap_blocks(zonal(mine, field_rows, ahead, ones, lat_count))
    adjoint = swap_blocks(zonal(mine, cotangent_rows, ahead, factor, lat_count))
    synthesis, saved = forward_middle(
        modes, channels, mixer,
        own_first.transpose(0, 2, 1), bias_lanes(first_bias),
        own_second.transpose(0, 2, 1), bias_lanes(second_bias),
    )
    mixed_modes = swap_blocks(synthesis)
    returned, grads = backward_middle(
        adjoint, channels, mixer, tall(own_first), tall(own_second), saved,
        1.0 / math.sqrt(row_count * KW),
    )
    return_modes = swap_blocks(returned)
    gradients = halve_gradients(grads).reshape(2, groups, 2 * width * width // lat_count)
    mixed = inverse(mixed_modes, back, factor, field_rows, True)
    field_gradient = inverse(return_modes, back, factor, cotangent_rows, False)
    return (grid_of(mixed), grid_of(field_gradient), gradients[0], gradients[1])


def gelu_value(values):
    tangent = jnp.tanh(GELU_SCALE * (values + GELU_CUBIC * values * values * values))
    return 0.5 * values * (1.0 + tangent)


def gelu_slope(values):
    tangent = jnp.tanh(GELU_SCALE * (values + GELU_CUBIC * values * values * values))
    inner = GELU_SCALE * (1.0 + 3.0 * GELU_CUBIC * values * values)
    return 0.5 * (1.0 + tangent) + 0.5 * values * (1.0 - tangent * tangent) * inner


def contract(pattern, former, latter):
    return jnp.einsum(pattern, former, latter, preferred_element_type=F32)


def complex_block(weights):
    width = weights.shape[1]
    real_part, imag_part = weights[:, :, :width], weights[:, :, width:]
    upper = jnp.stack([real_part, imag_part], axis=2)
    lower = jnp.stack([-imag_part, real_part], axis=2)
    return jnp.stack([upper, lower], axis=1)


def block_gradient(outer):
    real_part = outer[:, 0, :, 0, :] + outer[:, 1, :, 1, :]
    imag_part = outer[:, 0, :, 1, :] - outer[:, 1, :, 0, :]
    return jnp.concatenate([real_part, imag_part], axis=2)


def bias_layout(bias):
    groups, twice = bias.shape
    return bias.reshape(groups, 2, twice // 2).transpose(1, 0, 2)[None, :, None]


def plain(field, cotangent, first_weight, first_bias, second_weight, second_bias):
    local_rows, col_count, channels = field.shape
    width = first_weight.shape[1]
    groups = channels // width
    lat_count = lax.axis_size("lat")
    row_count = local_rows * lat_count
    ahead = jnp.asarray(zonal_waves(col_count, KW))
    factor = jnp.asarray(wave_factor(KW))
    cosine, sines = (jnp.asarray(t) for t in meridian_waves(row_count))
    forth = jnp.stack(
        [jnp.stack([cosine, sines], axis=-1), jnp.stack([-sines, cosine], axis=-1)], axis=1
    )
    first_block = complex_block(local_groups_of(first_weight, groups))
    second_block = complex_block(local_groups_of(second_weight, groups))

    def swap(array, split, concat):
        return lax.all_to_all(array, "lat", split_axis=split, concat_axis=concat, tiled=True)

    spectrum = contract("hwc,wrk->hrkc", field, ahead).astype(BF16)
    adjoint = (contract("hwc,wrk->hrkc", cotangent, ahead) * factor[:, None]).astype(BF16)
    modes, adjoint = swap(spectrum, 2, 0), swap(adjoint, 2, 0)
    block_shape = (row_count, 2, modes.shape[2], groups, width)
    inputs = contract("mphr,hrkc->mpkc", forth, modes).astype(BF16).reshape(block_shape)
    harmonic_adjoint = contract("mphr,hrkc->mpkc", forth, adjoint).reshape(block_shape)
    pre_first = contract("mrkgc,grcsd->mskgd", inputs, first_block) + bias_layout(
        local_groups_of(first_bias, groups)
    )
    hidden = gelu_value(pre_first).astype(BF16)
    pre_second = contract("mrkgc,grcsd->mskgd", hidden, second_block) + bias_layout(
        local_groups_of(second_bias, groups)
    )
    squashed = jnp.tanh(pre_second / SHRINK)
    shrunk = (pre_second - SHRINK * squashed).astype(BF16).reshape(modes.shape)
    second_adjoint = (harmonic_adjoint * (squashed * squashed)).astype(BF16)
    second_grad = block_gradient(contract("mrkgc,mskgd->grcsd", hidden, second_adjoint))
    hidden_adjoint = contract("mskgd,grcsd->mrkgc", second_adjoint, second_block)
    first_adjoint = (hidden_adjoint * gelu_slope(pre_first)).astype(BF16)
    first_grad = block_gradient(contract("mrkgc,mskgd->grcsd", inputs, first_adjoint))
    harmonics_adjoint = contract("mskgd,grcsd->mrkgc", first_adjoint, first_block).astype(BF16)
    synthesis = contract("mphr,mpkc->hrkc", forth, shrunk).astype(BF16)
    returned = contract(
        "mphr,mpkc->hrkc", forth, harmonics_adjoint.reshape(modes.shape)
    ).astype(BF16)
    mixed_modes, return_modes = swap(synthesis, 0, 2), swap(returned, 0, 2)
    gradients = reduce_gradients(
        jnp.stack([first_grad, second_grad]) * (1.0 / math.sqrt(row_count * KW)), lat_count
    )
    mixed_modes = (mixed_modes.astype(F32) * factor[:, None]).astype(BF16)
    mixed = (field.astype(F32) + contract("hrkc,wrk->hwc", mixed_modes, ahead)).astype(BF16)
    field_gradient = (
        cotangent.astype(F32) + contract("hrkc,wrk->hwc", return_modes, ahead)
    ).astype(BF16)
    return (mixed, field_gradient, gradients[0], gradients[1])


def on_device(field, *rest):
    local_rows, _, channels = field.shape
    lat_count = lax.axis_size("lat")
    fits = (
        KW == HALF * lat_count
        and channels % (2 * PACK) == 0
        and local_rows * lat_count % 2 == 0
        and rest[1].shape[1] % PACK == 0
        and local_rows * lat_count * PACK <= 512
        and lat_count & (lat_count - 1) == 0
        and rest[1].shape[1] // 2 % lat_count == 0
    )
    return (with_kernels if fits else plain)(field, *rest)


def solution(mesh):
    placed = (P(("rep", "lat"), None, "blk"), P(("rep", "lat"), None, "blk"), P(), P(), P(), P())
    return jax.shard_map(
        on_device,
        mesh=mesh,
        in_specs=placed,
        out_specs=(
            P(("rep", "lat"), None, "blk"),
            P(("rep", "lat"), None, "blk"),
            P(("rep", "blk"), "lat"),
            P(("rep", "blk"), "lat"),
        ),
        check_vma=False,
    )
```

```python
import functools
import math

import jax
import jax.numpy as jnp
import numpy as np
from jax import lax
from jax.experimental import pallas as pl
from jax.experimental.pallas import tpu as pltpu
from jax.sharding import PartitionSpec as P

KW = 512
LANES = 128
HALF = 64
PACK = 16
MIB = 1024 * 1024
ZONAL_MIB = 60
MIDDLE_MIB = 24
INVERSE_MIB = 24

SHRINK = 0.01
GELU_SCALE = 0.7978845608028654
GELU_CUBIC = 0.044715
F32 = jnp.float32
BF16 = jnp.bfloat16


def zonal_waves(col_count, kept):
    column = np.arange(col_count, dtype=np.int64)
    wavenumber = np.arange(kept, dtype=np.int64)
    phases = column[:, None] * wavenumber[None, :] % col_count
    angles = phases.astype(np.float32) * np.float32(2.0 * math.pi / col_count)
    scaling = np.float32(1.0 / math.sqrt(col_count))
    cosine = np.cos(angles) * scaling
    sines = np.sin(angles) * scaling
    return np.stack([cosine, -sines], axis=1).astype(BF16)


def meridian_waves(row_count):
    indices = np.arange(row_count, dtype=np.int64)
    phases = indices[:, None] * indices[None, :] % row_count
    angles = phases.astype(np.float32) * np.float32(2.0 * math.pi / row_count)
    scaling = np.float32(1.0 / math.sqrt(row_count))
    return ((np.cos(angles) * scaling).astype(BF16), (np.sin(angles) * scaling).astype(BF16))


def wave_factor(kept):
    return np.where(np.arange(kept) == 0, 1.0, 2.0).astype(np.float32)


def mm(former, latter):
    return jnp.dot(former, latter, preferred_element_type=F32)


def swap_parts(values, first_sign):
    lane = lax.broadcasted_iota(jnp.int32, (1, LANES), 1)
    sign = jnp.where(lane < HALF, first_sign, -first_sign).astype(F32)
    return pltpu.roll(values, HALF, axis=1) * sign


def slots(pieces):
    return (0, 7, 1, 6, 2, 5, 3, 4) if pieces == 8 else tuple(range(pieces))


def relative(mine, shift):
    return jnp.bitwise_xor(mine, shift)


def limits(mebibytes):
    return pltpu.CompilerParams(vmem_limit_bytes=mebibytes * MIB)


def zonal_kernel(mine_ref, field_ref, cotangent_ref, table_ref, scale_ref, *rest):
    outs, (rows_ref, pair_ref) = rest[:-2], rest[-2:]
    step = pl.program_id(0)
    lines, width, col_count = field_ref.shape
    half = lines * width

    @pl.when(step == 0)
    def _():
        rows_ref[:half] = field_ref[...].reshape(half, col_count)
        rows_ref[half:] = cotangent_ref[...].reshape(half, col_count)

    odd = jnp.bitwise_and(mine_ref[0], 1)
    result = mm(rows_ref[...], table_ref[...])
    for piece in range(2):
        lanes = slice(piece * LANES, (piece + 1) * LANES)
        pair_ref[piece, :half] = result[:half, lanes].astype(BF16)
        pair_ref[piece, half:] = (result[half:, lanes] * scale_ref[:, lanes]).astype(BF16)
    for place in range(len(outs) // 2):

        @pl.when(step == place)
        def _():
            where = slots(len(outs))
            outs[where.index(2 * place)][...] = pair_ref[odd]
            outs[where.index(2 * place + 1)][...] = pair_ref[1 - odd]


def zonal(mine, field, cotangent, table, scale, group, width, pieces):
    lines, _, col_count = field.shape
    rows = 2 * lines * width
    wide = 2 * LANES

    def block_of(i, place):
        return (0, jnp.bitwise_xor(lax.shift_right_logical(place[0], 1), i))

    own = pl.BlockSpec((lines, width, col_count), lambda i, place: (0, group, 0))
    return pl.pallas_call(
        zonal_kernel,
        grid_spec=pltpu.PrefetchScalarGridSpec(
            num_scalar_prefetch=1,
            grid=(pieces // 2,),
            in_specs=[
                own,
                own,
                pl.BlockSpec((col_count, wide), block_of),
                pl.BlockSpec((1, wide), block_of),
            ],
            out_specs=[pl.BlockSpec((rows, LANES), lambda i, place: (0, 0)) for _ in range(pieces)],
            scratch_shapes=[pltpu.VMEM((rows, col_count), BF16), pltpu.VMEM((2, rows, LANES), BF16)],
        ),
        out_shape=[jax.ShapeDtypeStruct((rows, LANES), BF16) for _ in range(pieces)],
        compiler_params=limits(ZONAL_MIB),
        cost_estimate=pl.CostEstimate(flops=4 * 10**9, bytes_accessed=4 * MIB, transcendentals=0),
    )(mine, field, cotangent, table, scale)


def inverse_kernel(pieces, given, group, *refs):
    blocks = refs[:pieces]
    table_ref, scale_ref, field_ref, cotangent_ref = refs[pieces : pieces + 4]
    before = refs[pieces + 4 : pieces + 4 + given]
    mixed_ref, gradient_ref, first_ref, second_ref, modes_ref = refs[pieces + 4 + given :]
    rows = modes_ref.shape[1]
    half = rows // 2

    @pl.when(pl.program_id(0) == 0)
    def _():
        mine = lax.axis_index("lat")
        for block, shift in zip(blocks, slots(pieces)):
            place = relative(mine, shift)
            scale = scale_ref[pl.ds(place, 1), :]
            modes_ref[place, :half] = (block[:half].astype(F32) * scale).astype(BF16)
            modes_ref[place, half:] = block[half:rows]
        total = blocks[0][rows:].astype(F32)
        for block in blocks[1:]:
            total += block[rows:].astype(F32)
        spread_gradient(total, 0, group, before[2:3], first_ref)
        spread_gradient(total, 1, group, before[3:4], second_ref)

    modes = jnp.concatenate([modes_ref[piece] for piece in range(pieces)], axis=1)
    result = mm(modes, table_ref[...])
    shape = field_ref.shape
    mixed_ref[...] = (field_ref[...].astype(F32) + result[:half].reshape(shape)).astype(BF16)
    gradient_ref[...] = (cotangent_ref[...].astype(F32) + result[half:].reshape(shape)).astype(BF16)


def spread_gradient(total, kind, group, before, out_ref):
    for member in range(group):
        out_ref[member : member + 1] = before[0][member : member + 1]
    lines = []
    for line in range(out_ref.shape[1] // (LANES + HALF)):
        lines.append(total[kind * PACK + line : kind * PACK + line + 1])
        lines.append(total[2 * PACK + line : 2 * PACK + line + 1, kind * HALF : (kind + 1) * HALF])
    out_ref[group : group + 1] = jnp.concatenate(lines, axis=1)


def pack_gradients(sums_ref, packed_ref):
    pieces = packed_ref.shape[0]
    part = (sums_ref.shape[1] - PACK) // pieces
    for piece in range(pieces):
        lines = slice(piece * part, piece * part + PACK)
        both = [sums_ref[kind, lines, :] for kind in range(2)]
        for kind in range(2):
            packed_ref[piece, kind * PACK : (kind + 1) * PACK] = both[kind][:, :LANES].astype(BF16)
        tails = jnp.concatenate([value[:, LANES:] for value in both], axis=1)
        packed_ref[piece, 2 * PACK :] = tails.astype(BF16)


def inverse(blocks, table, scale, field, cotangent, group, groups, gradient_size, before):
    pieces = len(blocks)
    kept, col_count = table.shape
    lines, channels, _ = field.shape
    width = channels // groups
    rows = 2 * lines * width
    wide = 512
    own = pl.BlockSpec((lines, width, wide), lambda i: (0, group, i))
    anywhere = pl.BlockSpec(memory_space=pl.ANY)
    gradient = pl.BlockSpec((groups, gradient_size), lambda i: (0, 0))
    return pl.pallas_call(
        functools.partial(inverse_kernel, pieces, len(before), group),
        grid=(pl.cdiv(col_count, wide),),
        in_specs=[pl.BlockSpec(block.shape, lambda i: (0, 0)) for block in blocks]
        + [
            pl.BlockSpec((kept, wide), lambda i: (0, i)),
            pl.BlockSpec(scale.shape, lambda i: (0, 0)),
            own,
            own,
        ]
        + ([anywhere, anywhere, gradient, gradient] if before else []),
        out_specs=[own, own, gradient, gradient],
        out_shape=[jax.ShapeDtypeStruct(field.shape, BF16) for _ in range(2)]
        + [jax.ShapeDtypeStruct((groups, gradient_size), F32) for _ in range(2)],
        scratch_shapes=[pltpu.VMEM((pieces, rows, LANES), BF16)],
        input_output_aliases={pieces + 4 + i: i for i in range(2)} if before else {},
        compiler_params=limits(INVERSE_MIB),
        cost_estimate=pl.CostEstimate(flops=4 * 10**9, bytes_accessed=5 * MIB, transcendentals=0),
    )(*blocks, table, scale, field, cotangent, *before)


def meridian(load, mixer, first_sign, channels, store):
    count = mixer.shape[1] // PACK
    for start in range(0, channels, 2 * PACK):
        pair = jnp.concatenate(
            [load(start + shift).reshape(count * PACK, LANES) for shift in (0, PACK)], axis=1
        )
        both = mm(mixer[...], pair)
        for index in range(2):
            half = both[:, index * LANES : (index + 1) * LANES]
            value = half[: count * PACK] + swap_parts(half[count * PACK :], first_sign)
            store(start + index * PACK, value.reshape(count, PACK, LANES))


def complex_dot(weights, operand, first_sign):
    width = weights.shape[0] // 2
    both = mm(weights, jnp.concatenate(operand, axis=1))
    return [
        both[:width, i * LANES : (i + 1) * LANES]
        + swap_parts(both[width:, i * LANES : (i + 1) * LANES], first_sign)
        for i in range(len(operand))
    ]


def nt(former, latter):
    return lax.dot_general(former, latter, (((1,), (1,)), ((), ())), preferred_element_type=F32)


def side_by_side(pieces):
    return jnp.concatenate(pieces, axis=1)


def bias_lanes(bias_ref, index):
    tall = jnp.broadcast_to(bias_ref[pl.ds(index, 1), :], (LANES, bias_ref.shape[1])).T
    width = bias_ref.shape[1] // 2
    lane = lax.broadcasted_iota(jnp.int32, (1, LANES), 1)
    return jnp.where(lane < HALF, tall[:width], tall[width:])


def stacked(weight):
    width = weight.shape[0]
    return jnp.concatenate([weight[:, :width], weight[:, width:]], axis=0)


def middle_kernel(group, groups, normalizer, pieces, *refs):
    blocks, refs = refs[:pieces], refs[pieces:]
    (mixer_ref, first_ref, first_bias_ref, second_ref, second_bias_ref), refs = refs[:5], refs[5:]
    outs, refs = refs[:pieces], refs[pieces:]
    modes_ref, adjoint_ref, harm_ref, shrunk_ref, exact_ref, sums_ref, packed_ref = refs
    mine = lax.axis_index("lat")
    index = lax.axis_index("blk") * groups + group
    count, width, _ = modes_ref.shape
    lines = count // pieces
    for block, shift in zip(blocks, slots(pieces)):
        for line in range(lines):
            row = relative(mine, shift) * lines + line
            modes_ref[row] = block[line * width : (line + 1) * width]
            adjoint_ref[row] = block[(lines + line) * width : (lines + line + 1) * width]

    first, second = first_ref[index], second_ref[index]
    first_ahead, second_ahead = first.T, second.T
    first_back, second_back = stacked(first), stacked(second)
    first_bias, second_bias = bias_lanes(first_bias_ref, index), bias_lanes(second_bias_ref, index)

    def keep(start, value):
        harm_ref[:, start : start + PACK, :] = value.astype(BF16)

    meridian(lambda c: modes_ref[:, c : c + PACK, :], mixer_ref, 1.0, width, keep)

    def keep_adjoint(start, value):
        exact_ref[:, start : start + PACK, :] = value

    meridian(lambda c: adjoint_ref[:, c : c + PACK, :], mixer_ref, 1.0, width, keep_adjoint)

    first_sum = jnp.zeros((width, 2 * width), F32)
    second_sum = jnp.zeros((width, 2 * width), F32)
    for row in range(0, count, 2):
        both = range(2)
        inputs = [harm_ref[row + i] for i in both]
        pre = complex_dot(first_ahead, inputs, -1.0)
        hidden, slope = [], []
        for i in both:
            v = pre[i] + first_bias
            square = v * v
            tangent = jnp.tanh(GELU_SCALE * (v + GELU_CUBIC * square * v))
            outer = 0.5 * (1.0 + tangent)
            inner = GELU_SCALE * (1.0 + 3.0 * GELU_CUBIC * square)
            hidden.append((v * outer).astype(BF16))
            slope.append(outer + 0.5 * v * (1.0 - tangent * tangent) * inner)
        pre = complex_dot(second_ahead, hidden, -1.0)
        exact = []
        for i in both:
            v = pre[i] + second_bias
            squashed = jnp.tanh(v * (1.0 / SHRINK))
            shrunk_ref[row + i] = (v - SHRINK * squashed).astype(BF16)
            exact.append(exact_ref[row + i] * (squashed * squashed))
        second_adjoint = [a.astype(BF16) for a in exact]
        turned = [swap_parts(a, 1.0).astype(BF16) for a in exact]
        pairs = jnp.concatenate([side_by_side(second_adjoint), side_by_side(turned)], axis=0)
        second_sum += nt(side_by_side(hidden), pairs)
        back = complex_dot(second_back, second_adjoint, 1.0)
        exact = [back[i] * slope[i] for i in both]
        first_adjoint = [a.astype(BF16) for a in exact]
        turned = [swap_parts(a, 1.0).astype(BF16) for a in exact]
        pairs = jnp.concatenate([side_by_side(first_adjoint), side_by_side(turned)], axis=0)
        first_sum += nt(side_by_side(inputs), pairs)
        back = complex_dot(first_back, first_adjoint, 1.0)
        for i in both:
            harm_ref[row + i] = back[i].astype(BF16)

    sums_ref[0, :width] = first_sum * normalizer
    sums_ref[1, :width] = second_sum * normalizer
    sums_ref[:, width:] = jnp.zeros((2, PACK, 2 * width), F32)
    pack_gradients(sums_ref, packed_ref)

    def emit(start, value):
        modes_ref[:, start : start + PACK, :] = value.astype(BF16)

    def emit_adjoint(start, value):
        adjoint_ref[:, start : start + PACK, :] = value.astype(BF16)

    meridian(lambda c: shrunk_ref[:, c : c + PACK, :], mixer_ref, -1.0, width, emit)
    meridian(lambda c: harm_ref[:, c : c + PACK, :], mixer_ref, -1.0, width, emit_adjoint)
    for out, shift in zip(outs, slots(pieces)):
        for line in range(lines):
            row = relative(mine, shift) * lines + line
            out[line * width : (line + 1) * width] = modes_ref[row]
            out[(lines + line) * width : (lines + line + 1) * width] = adjoint_ref[row]
        out[2 * lines * width :] = packed_ref[relative(mine, shift)]


def whole(*shape):
    return pl.BlockSpec(shape, lambda: (0,) * len(shape))


def middle(blocks, lines, mixer, first, first_bias, second, second_bias, group, groups, normalizer):
    pieces = len(blocks)
    width = first.shape[1]
    shape = (pieces * lines, width, LANES)
    operands = (*blocks, mixer, first, first_bias, second, second_bias)
    longer = (blocks[0].shape[0] + 3 * PACK, LANES)
    return pl.pallas_call(
        functools.partial(middle_kernel, group, groups, normalizer, pieces),
        in_specs=[whole(*a.shape) for a in operands],
        out_specs=[whole(*longer) for _ in blocks],
        out_shape=[jax.ShapeDtypeStruct(longer, BF16) for _ in blocks],
        scratch_shapes=[pltpu.VMEM(shape, BF16) for _ in range(4)]
        + [
            pltpu.VMEM(shape, F32),
            pltpu.VMEM((2, width + PACK, 2 * width), F32),
            pltpu.VMEM((pieces, 3 * PACK, LANES), BF16),
        ],
        compiler_params=limits(MIDDLE_MIB),
        cost_estimate=pl.CostEstimate(flops=7 * 10**9, bytes_accessed=4 * MIB, transcendentals=0),
    )(*operands)


def local_groups_of(array, groups):
    return lax.dynamic_slice_in_dim(array, lax.axis_index("blk") * groups, groups, axis=0)


def exchange(blocks):
    return lax.all_to_all(blocks, "lat", split_axis=0, concat_axis=0, tiled=True)


def pass_to(block, shift):
    count = lax.axis_size("lat")
    return lax.ppermute(block, "lat", [(place, place ^ shift) for place in range(count)])


def swap_blocks(blocks):
    return [pass_to(block, shift) if shift else block for block, shift in zip(blocks, slots(len(blocks)))]


def reduce_gradients(grads, lat_count):
    kinds, groups, width, twice = grads.shape
    piece = width * twice // lat_count
    split = grads.reshape(kinds * groups, lat_count, piece).transpose(1, 0, 2)
    if kinds * groups * piece % LANES == 0:
        split = split.reshape(lat_count, kinds * groups * piece // LANES, LANES)
    total = jnp.sum(exchange(split), axis=0)
    return total.reshape(kinds, groups, piece)


def with_kernels(field, cotangent, first_weight, first_bias, second_weight, second_bias):
    local_rows, col_count, channels = field.shape
    width = first_weight.shape[1]
    groups = channels // width
    lat_count = lax.axis_size("lat")
    row_count = local_rows * lat_count
    sub_count = KW // lat_count
    waves = zonal_waves(col_count, KW)
    table = (
        waves.reshape(col_count, 2, lat_count, sub_count).transpose(0, 2, 1, 3).reshape(col_count, 2 * KW)
    )
    factor = np.repeat(wave_factor(KW).reshape(lat_count, 1, sub_count), 2, axis=1)
    cosine, sines = meridian_waves(row_count)
    unit = np.eye(PACK, dtype=np.float32)
    mixer = np.concatenate(
        [np.kron(cosine.astype(np.float32), unit), np.kron(sines.astype(np.float32), unit)], axis=0
    ).astype(BF16)
    ahead, back = jnp.asarray(table), jnp.asarray(np.ascontiguousarray(table.T))
    wide_factor = jnp.asarray(factor.reshape(1, 2 * KW))
    tall_factor = jnp.asarray(factor.reshape(lat_count, 2 * sub_count))
    mixer = jnp.asarray(mixer)
    normalizer = 1.0 / math.sqrt(row_count * KW)
    mine = lax.axis_index("lat").astype(jnp.int32).reshape(1)
    field, cotangent = field.transpose(0, 2, 1), cotangent.transpose(0, 2, 1)

    arrived = [
        swap_blocks(zonal(mine, field, cotangent, ahead, wide_factor, group, width, lat_count))
        for group in range(groups)
    ]
    returned = [
        swap_blocks(
            middle(
                arrived[group], local_rows, mixer, first_weight, first_bias, second_weight, second_bias,
                group, groups, normalizer,
            )
        )
        for group in range(groups)
    ]
    results = []
    for group in range(groups):
        results = inverse(
            returned[group], back, tall_factor, field, cotangent, group, groups,
            2 * width * width // lat_count, results,
        )
    mixed, field_gradient = (result.transpose(0, 2, 1) for result in results[:2])
    return (mixed, field_gradient, results[2], results[3])


def gelu_value(values):
    tangent = jnp.tanh(GELU_SCALE * (values + GELU_CUBIC * values * values * values))
    return 0.5 * values * (1.0 + tangent)


def gelu_slope(values):
    tangent = jnp.tanh(GELU_SCALE * (values + GELU_CUBIC * values * values * values))
    inner = GELU_SCALE * (1.0 + 3.0 * GELU_CUBIC * values * values)
    return 0.5 * (1.0 + tangent) + 0.5 * values * (1.0 - tangent * tangent) * inner


def contract(pattern, former, latter):
    return jnp.einsum(pattern, former, latter, preferred_element_type=F32)


def complex_block(weights):
    width = weights.shape[1]
    real_part, imag_part = weights[:, :, :width], weights[:, :, width:]
    upper = jnp.stack([real_part, imag_part], axis=2)
    lower = jnp.stack([-imag_part, real_part], axis=2)
    return jnp.stack([upper, lower], axis=1)


def block_gradient(outer):
    real_part = outer[:, 0, :, 0, :] + outer[:, 1, :, 1, :]
    imag_part = outer[:, 0, :, 1, :] - outer[:, 1, :, 0, :]
    return jnp.concatenate([real_part, imag_part], axis=2)


def bias_layout(bias):
    groups, twice = bias.shape
    return bias.reshape(groups, 2, twice // 2).transpose(1, 0, 2)[None, :, None]


def plain(field, cotangent, first_weight, first_bias, second_weight, second_bias):
    local_rows, col_count, channels = field.shape
    width = first_weight.shape[1]
    groups = channels // width
    lat_count = lax.axis_size("lat")
    row_count = local_rows * lat_count
    ahead = jnp.asarray(zonal_waves(col_count, KW))
    factor = jnp.asarray(wave_factor(KW))
    cosine, sines = (jnp.asarray(t) for t in meridian_waves(row_count))
    forth = jnp.stack(
        [jnp.stack([cosine, sines], axis=-1), jnp.stack([-sines, cosine], axis=-1)], axis=1
    )
    first_block = complex_block(local_groups_of(first_weight, groups))
    second_block = complex_block(local_groups_of(second_weight, groups))

    def swap(array, split, concat):
        return lax.all_to_all(array, "lat", split_axis=split, concat_axis=concat, tiled=True)

    spectrum = contract("hwc,wrk->hrkc", field, ahead).astype(BF16)
    adjoint = (contract("hwc,wrk->hrkc", cotangent, ahead) * factor[:, None]).astype(BF16)
    modes, adjoint = swap(spectrum, 2, 0), swap(adjoint, 2, 0)
    block_shape = (row_count, 2, modes.shape[2], groups, width)
    inputs = contract("mphr,hrkc->mpkc", forth, modes).astype(BF16).reshape(block_shape)
    harmonic_adjoint = contract("mphr,hrkc->mpkc", forth, adjoint).reshape(block_shape)
    pre_first = contract("mrkgc,grcsd->mskgd", inputs, first_block) + bias_layout(
        local_groups_of(first_bias, groups)
    )
    hidden = gelu_value(pre_first).astype(BF16)
    pre_second = contract("mrkgc,grcsd->mskgd", hidden, second_block) + bias_layout(
        local_groups_of(second_bias, groups)
    )
    squashed = jnp.tanh(pre_second / SHRINK)
    shrunk = (pre_second - SHRINK * squashed).astype(BF16).reshape(modes.shape)
    second_adjoint = (harmonic_adjoint * (squashed * squashed)).astype(BF16)
    second_grad = block_gradient(contract("mrkgc,mskgd->grcsd", hidden, second_adjoint))
    hidden_adjoint = contract("mskgd,grcsd->mrkgc", second_adjoint, second_block)
    first_adjoint = (hidden_adjoint * gelu_slope(pre_first)).astype(BF16)
    first_grad = block_gradient(contract("mrkgc,mskgd->grcsd", inputs, first_adjoint))
    harmonics_adjoint = contract("mskgd,grcsd->mrkgc", first_adjoint, first_block).astype(BF16)
    synthesis = contract("mphr,mpkc->hrkc", forth, shrunk).astype(BF16)
    returned = contract(
        "mphr,mpkc->hrkc", forth, harmonics_adjoint.reshape(modes.shape)
    ).astype(BF16)
    mixed_modes, return_modes = swap(synthesis, 0, 2), swap(returned, 0, 2)
    gradients = reduce_gradients(
        jnp.stack([first_grad, second_grad]) * (1.0 / math.sqrt(row_count * KW)), lat_count
    )
    mixed_modes = (mixed_modes.astype(F32) * factor[:, None]).astype(BF16)
    mixed = (field.astype(F32) + contract("hrkc,wrk->hwc", mixed_modes, ahead)).astype(BF16)
    field_gradient = (
        cotangent.astype(F32) + contract("hrkc,wrk->hwc", return_modes, ahead)
    ).astype(BF16)
    return (mixed, field_gradient, gradients[0], gradients[1])


def on_device(field, *rest):
    local_rows, _, channels = field.shape
    lat_count = lax.axis_size("lat")
    fits = (
        KW == HALF * lat_count
        and channels == 2 * rest[1].shape[1]
        and local_rows * lat_count % 2 == 0
        and rest[1].shape[1] % (2 * PACK) == 0
        and local_rows * lat_count * PACK <= 512
        and lat_count & (lat_count - 1) == 0
        and rest[1].shape[1] % lat_count == 0
        and rest[1].shape[1] // lat_count <= PACK
        and 2 * rest[1].shape[1] == LANES + HALF
    )
    return (with_kernels if fits else plain)(field, *rest)


def solution(mesh):
    placed = (P(("rep", "lat"), None, "blk"), P(("rep", "lat"), None, "blk"), P(), P(), P(), P())
    return jax.shard_map(
        on_device,
        mesh=mesh,
        in_specs=placed,
        out_specs=(
            P(("rep", "lat"), None, "blk"),
            P(("rep", "lat"), None, "blk"),
            P(("rep", "blk"), "lat"),
            P(("rep", "blk"), "lat"),
        ),
        check_vma=False,
    )
```

```python
import functools
import math

import jax
import jax.numpy as jnp
import numpy as np
from jax import lax
from jax.experimental import pallas as pl
from jax.experimental.pallas import tpu as pltpu
from jax.sharding import PartitionSpec as P

KW = 512
LANES = 128
HALF = 64
PACK = 16
MIB = 1024 * 1024
ZONAL_MIB = 24
MIDDLE_MIB = 24
INVERSE_MIB = 24

SHRINK = 0.01
GELU_SCALE = 0.7978845608028654
GELU_CUBIC = 0.044715
F32 = jnp.float32
BF16 = jnp.bfloat16


def zonal_waves(col_count, kept):
    column = np.arange(col_count, dtype=np.int64)
    wavenumber = np.arange(kept, dtype=np.int64)
    phases = column[:, None] * wavenumber[None, :] % col_count
    angles = phases.astype(np.float32) * np.float32(2.0 * math.pi / col_count)
    scaling = np.float32(1.0 / math.sqrt(col_count))
    cosine = np.cos(angles) * scaling
    sines = np.sin(angles) * scaling
    return np.stack([cosine, -sines], axis=1).astype(BF16)


def meridian_waves(row_count):
    indices = np.arange(row_count, dtype=np.int64)
    phases = indices[:, None] * indices[None, :] % row_count
    angles = phases.astype(np.float32) * np.float32(2.0 * math.pi / row_count)
    scaling = np.float32(1.0 / math.sqrt(row_count))
    return ((np.cos(angles) * scaling).astype(BF16), (np.sin(angles) * scaling).astype(BF16))


def wave_factor(kept):
    return np.where(np.arange(kept) == 0, 1.0, 2.0).astype(np.float32)


def mm(former, latter):
    return jnp.dot(former, latter, preferred_element_type=F32)


def with_swapped(values, first_sign):
    lane = lax.broadcasted_iota(jnp.int32, (1, LANES), 1)
    sign = jnp.where(lane < HALF, first_sign, -first_sign).astype(values.dtype)
    return jnp.concatenate([values, pltpu.roll(values, HALF, axis=1) * sign], axis=0)


def slots(pieces):
    return (0, 7, 1, 6, 2, 5, 3, 4) if pieces == 8 else tuple(range(pieces))


def relative(mine, shift):
    return jnp.bitwise_xor(mine, shift)


def limits(mebibytes):
    return pltpu.CompilerParams(vmem_limit_bytes=mebibytes * MIB)


def zonal_kernel(group, width, pieces, field_ref, cotangent_ref, table_ref, scale_ref, *refs):
    outs, (rows_ref, columns_ref, pair_ref, row_sems, column_sems) = refs[:pieces], refs[pieces:]
    lines = field_ref.shape[0]
    half = lines * width
    wide = 2 * LANES
    mine = lax.axis_index("lat")
    pair = lax.shift_right_logical(mine, 1)
    odd = jnp.bitwise_and(mine, 1)
    rows = []
    for kind, source in enumerate((field_ref, cotangent_ref)):
        for line in range(lines):
            index = kind * lines + line
            copy = pltpu.make_async_copy(
                source.at[line, group * width : (group + 1) * width, :],
                rows_ref.at[index * width : (index + 1) * width, :],
                row_sems.at[index],
            )
            copy.start()
            rows.append(copy)
    columns = []
    for place in range(pieces // 2):
        begin = pl.multiple_of(jnp.bitwise_xor(pair, place) * wide, wide)
        copy = pltpu.make_async_copy(
            table_ref.at[:, pl.ds(begin, wide)], columns_ref.at[place], column_sems.at[place]
        )
        copy.start()
        columns.append(copy)
    for copy in rows:
        copy.wait()
    where = slots(pieces)
    for place in range(pieces // 2):
        columns[place].wait()
        result = mm(rows_ref[...], columns_ref[place])
        for piece in range(2):
            lanes = slice(piece * LANES, (piece + 1) * LANES)
            scale = scale_ref[pl.ds(2 * jnp.bitwise_xor(pair, place) + piece, 1), :]
            pair_ref[piece, :half] = result[:half, lanes].astype(BF16)
            pair_ref[piece, half:] = (result[half:, lanes] * scale).astype(BF16)
        outs[where.index(2 * place)][...] = pair_ref[odd]
        outs[where.index(2 * place + 1)][...] = pair_ref[1 - odd]


def zonal(field, cotangent, table, scale, group, width, pieces):
    lines, _, col_count = field.shape
    rows = 2 * lines * width
    away = pl.BlockSpec(memory_space=pltpu.HBM)
    return pl.pallas_call(
        functools.partial(zonal_kernel, group, width, pieces),
        in_specs=[away, away, away, whole(*scale.shape)],
        out_specs=[whole(rows, LANES) for _ in range(pieces)],
        out_shape=[jax.ShapeDtypeStruct((rows, LANES), BF16) for _ in range(pieces)],
        scratch_shapes=[
            pltpu.VMEM((rows, col_count), BF16),
            pltpu.VMEM((pieces // 2, col_count, 2 * LANES), BF16),
            pltpu.VMEM((2, rows, LANES), BF16),
            pltpu.SemaphoreType.DMA((2 * lines,)),
            pltpu.SemaphoreType.DMA((pieces // 2,)),
        ],
        compiler_params=limits(ZONAL_MIB),
        cost_estimate=pl.CostEstimate(flops=4 * 10**9, bytes_accessed=4 * MIB, transcendentals=0),
    )(field, cotangent, table, scale)


def inverse_kernel(pieces, given, group, *refs):
    blocks = refs[:pieces]
    table_ref, scale_ref, field_ref, cotangent_ref = refs[pieces : pieces + 4]
    before = refs[pieces + 4 : pieces + 4 + given]
    mixed_ref, gradient_ref, first_ref, second_ref, modes_ref = refs[pieces + 4 + given :]
    rows = modes_ref.shape[1]
    half = rows // 2

    @pl.when(pl.program_id(0) == 0)
    def _():
        mine = lax.axis_index("lat")
        for block, shift in zip(blocks, slots(pieces)):
            place = relative(mine, shift)
            scale = scale_ref[pl.ds(place, 1), :]
            modes_ref[place, :half] = (block[:half].astype(F32) * scale).astype(BF16)
            modes_ref[place, half:] = block[half:rows]
        total = blocks[0][rows:].astype(F32)
        for block in blocks[1:]:
            total += block[rows:].astype(F32)
        spread_gradient(total, 0, group, before[2:3], first_ref)
        spread_gradient(total, 1, group, before[3:4], second_ref)

    modes = jnp.concatenate([modes_ref[piece] for piece in range(pieces)], axis=1)
    result = mm(modes, table_ref[...])
    shape = field_ref.shape
    mixed_ref[...] = (field_ref[...].astype(F32) + result[:half].reshape(shape)).astype(BF16)
    gradient_ref[...] = (cotangent_ref[...].astype(F32) + result[half:].reshape(shape)).astype(BF16)


def spread_gradient(total, kind, group, before, out_ref):
    for member in range(group):
        out_ref[member : member + 1] = before[0][member : member + 1]
    lines = []
    for line in range(out_ref.shape[1] // (LANES + HALF)):
        lines.append(total[kind * PACK + line : kind * PACK + line + 1])
        lines.append(total[2 * PACK + line : 2 * PACK + line + 1, kind * HALF : (kind + 1) * HALF])
    out_ref[group : group + 1] = jnp.concatenate(lines, axis=1)


def pack_gradients(sums_ref, packed_ref):
    pieces = packed_ref.shape[0]
    part = (sums_ref.shape[1] - PACK) // pieces
    for piece in range(pieces):
        lines = slice(piece * part, piece * part + PACK)
        both = [sums_ref[kind, lines, :] for kind in range(2)]
        for kind in range(2):
            packed_ref[piece, kind * PACK : (kind + 1) * PACK] = both[kind][:, :LANES].astype(BF16)
        tails = jnp.concatenate([value[:, LANES:] for value in both], axis=1)
        packed_ref[piece, 2 * PACK :] = tails.astype(BF16)


def inverse(blocks, table, scale, field, cotangent, group, groups, gradient_size, before):
    pieces = len(blocks)
    kept, col_count = table.shape
    lines, channels, _ = field.shape
    width = channels // groups
    rows = 2 * lines * width
    wide = 512
    own = pl.BlockSpec((lines, width, wide), lambda i: (0, group, i))
    anywhere = pl.BlockSpec(memory_space=pl.ANY)
    gradient = pl.BlockSpec((groups, gradient_size), lambda i: (0, 0))
    return pl.pallas_call(
        functools.partial(inverse_kernel, pieces, len(before), group),
        grid=(pl.cdiv(col_count, wide),),
        in_specs=[pl.BlockSpec(block.shape, lambda i: (0, 0)) for block in blocks]
        + [
            pl.BlockSpec((kept, wide), lambda i: (0, i)),
            pl.BlockSpec(scale.shape, lambda i: (0, 0)),
            own,
            own,
        ]
        + ([anywhere, anywhere, gradient, gradient] if before else []),
        out_specs=[own, own, gradient, gradient],
        out_shape=[jax.ShapeDtypeStruct(field.shape, BF16) for _ in range(2)]
        + [jax.ShapeDtypeStruct((groups, gradient_size), F32) for _ in range(2)],
        scratch_shapes=[pltpu.VMEM((pieces, rows, LANES), BF16)],
        input_output_aliases={pieces + 4 + i: i for i in range(2)} if before else {},
        compiler_params=limits(INVERSE_MIB),
        cost_estimate=pl.CostEstimate(flops=4 * 10**9, bytes_accessed=5 * MIB, transcendentals=0),
    )(*blocks, table, scale, field, cotangent, *before)


def meridian(load, mixer, first_sign, channels, store):
    count = mixer.shape[0] // PACK
    for start in range(0, channels, 2 * PACK):
        pair = [
            with_swapped(load(start + shift).reshape(count * PACK, LANES), first_sign)
            for shift in (0, PACK)
        ]
        both = mm(mixer[...], side_by_side(pair))
        for index in range(2):
            value = both[:, index * LANES : (index + 1) * LANES]
            store(start + index * PACK, value.reshape(count, PACK, LANES))


def nt(former, latter):
    return lax.dot_general(former, latter, (((1,), (1,)), ((), ())), preferred_element_type=F32)


def side_by_side(pieces):
    return jnp.concatenate(pieces, axis=1)


def bias_lanes(bias_ref, index):
    tall = jnp.broadcast_to(bias_ref[pl.ds(index, 1), :], (LANES, bias_ref.shape[1])).T
    width = bias_ref.shape[1] // 2
    lane = lax.broadcasted_iota(jnp.int32, (1, LANES), 1)
    return jnp.where(lane < HALF, tall[:width], tall[width:])


def forth(weight):
    width = weight.shape[0]
    turned = weight.T
    return side_by_side([turned[:width], turned[width:]])


def middle_kernel(group, groups, normalizer, pieces, *refs):
    blocks, refs = refs[:pieces], refs[pieces:]
    (mixer_ref, first_ref, first_bias_ref, second_ref, second_bias_ref), refs = refs[:5], refs[5:]
    outs, refs = refs[:pieces], refs[pieces:]
    modes_ref, adjoint_ref, harm_ref, shrunk_ref, exact_ref, sums_ref, packed_ref = refs
    mine = lax.axis_index("lat")
    index = lax.axis_index("blk") * groups + group
    count, width, _ = modes_ref.shape
    lines = count // pieces
    for block, shift in zip(blocks, slots(pieces)):
        for line in range(lines):
            row = relative(mine, shift) * lines + line
            modes_ref[row] = block[line * width : (line + 1) * width]
            adjoint_ref[row] = block[(lines + line) * width : (lines + line + 1) * width]

    first, second = first_ref[index], second_ref[index]
    first_ahead, second_ahead = forth(first), forth(second)
    first_bias, second_bias = bias_lanes(first_bias_ref, index), bias_lanes(second_bias_ref, index)

    def keep(start, value):
        harm_ref[:, start : start + PACK, :] = value.astype(BF16)

    meridian(lambda c: modes_ref[:, c : c + PACK, :], mixer_ref, 1.0, width, keep)

    def keep_adjoint(start, value):
        exact_ref[:, start : start + PACK, :] = value

    meridian(lambda c: adjoint_ref[:, c : c + PACK, :], mixer_ref, 1.0, width, keep_adjoint)

    first_sum = jnp.zeros((width, 2 * width), F32)
    second_sum = jnp.zeros((width, 2 * width), F32)
    step = 2
    for row in range(0, count, step):
        members = range(step)

        def lanes_of(wide):
            return [wide[:, i * LANES : (i + 1) * LANES] for i in members]

        inputs = [harm_ref[row + i] for i in members]
        pre = lanes_of(mm(first_ahead, side_by_side([with_swapped(x, -1.0) for x in inputs])))
        hidden, slope = [], []
        for i in members:
            v = pre[i] + first_bias
            square = v * v
            tangent = jnp.tanh(v * (GELU_SCALE + GELU_SCALE * GELU_CUBIC * square))
            outer = 0.5 + 0.5 * tangent
            inner = 0.5 * GELU_SCALE + 1.5 * GELU_SCALE * GELU_CUBIC * square
            hidden.append((v * outer).astype(BF16))
            slope.append(outer + v * (1.0 - tangent * tangent) * inner)
        pre = lanes_of(mm(second_ahead, side_by_side([with_swapped(x, -1.0) for x in hidden])))
        second_adjoint = []
        for i in members:
            v = pre[i] + second_bias
            squashed = jnp.tanh(v * (1.0 / SHRINK))
            shrunk_ref[row + i] = (v - SHRINK * squashed).astype(BF16)
            second_adjoint.append((exact_ref[row + i] * (squashed * squashed)).astype(BF16))
        pairs = side_by_side([with_swapped(x, 1.0) for x in second_adjoint])
        second_sum += nt(side_by_side(hidden), pairs)
        back = lanes_of(mm(second, pairs))
        first_adjoint = [(back[i] * slope[i]).astype(BF16) for i in members]
        pairs = side_by_side([with_swapped(x, 1.0) for x in first_adjoint])
        first_sum += nt(side_by_side(inputs), pairs)
        back = lanes_of(mm(first, pairs))
        for i in members:
            harm_ref[row + i] = back[i].astype(BF16)

    sums_ref[0, :width] = first_sum * normalizer
    sums_ref[1, :width] = second_sum * normalizer
    sums_ref[:, width:] = jnp.zeros((2, PACK, 2 * width), F32)
    pack_gradients(sums_ref, packed_ref)

    def emit(start, value):
        modes_ref[:, start : start + PACK, :] = value.astype(BF16)

    def emit_adjoint(start, value):
        adjoint_ref[:, start : start + PACK, :] = value.astype(BF16)

    meridian(lambda c: shrunk_ref[:, c : c + PACK, :], mixer_ref, -1.0, width, emit)
    meridian(lambda c: harm_ref[:, c : c + PACK, :], mixer_ref, -1.0, width, emit_adjoint)
    for out, shift in zip(outs, slots(pieces)):
        for line in range(lines):
            row = relative(mine, shift) * lines + line
            out[line * width : (line + 1) * width] = modes_ref[row]
            out[(lines + line) * width : (lines + line + 1) * width] = adjoint_ref[row]
        out[2 * lines * width :] = packed_ref[relative(mine, shift)]


def whole(*shape):
    return pl.BlockSpec(shape, lambda: (0,) * len(shape))


def middle(blocks, lines, mixer, first, first_bias, second, second_bias, group, groups, normalizer):
    pieces = len(blocks)
    width = first.shape[1]
    shape = (pieces * lines, width, LANES)
    operands = (*blocks, mixer, first, first_bias, second, second_bias)
    longer = (blocks[0].shape[0] + 3 * PACK, LANES)
    return pl.pallas_call(
        functools.partial(middle_kernel, group, groups, normalizer, pieces),
        in_specs=[whole(*a.shape) for a in operands],
        out_specs=[whole(*longer) for _ in blocks],
        out_shape=[jax.ShapeDtypeStruct(longer, BF16) for _ in blocks],
        scratch_shapes=[pltpu.VMEM(shape, BF16) for _ in range(4)]
        + [
            pltpu.VMEM(shape, F32),
            pltpu.VMEM((2, width + PACK, 2 * width), F32),
            pltpu.VMEM((pieces, 3 * PACK, LANES), BF16),
        ],
        compiler_params=limits(MIDDLE_MIB),
        cost_estimate=pl.CostEstimate(flops=7 * 10**9, bytes_accessed=4 * MIB, transcendentals=0),
    )(*operands)


def local_groups_of(array, groups):
    return lax.dynamic_slice_in_dim(array, lax.axis_index("blk") * groups, groups, axis=0)


def exchange(blocks):
    return lax.all_to_all(blocks, "lat", split_axis=0, concat_axis=0, tiled=True)


def pass_to(block, shift):
    count = lax.axis_size("lat")
    return lax.ppermute(block, "lat", [(place, place ^ shift) for place in range(count)])


def swap_blocks(blocks):
    return [pass_to(block, shift) if shift else block for block, shift in zip(blocks, slots(len(blocks)))]


def reduce_gradients(grads, lat_count):
    kinds, groups, width, twice = grads.shape
    piece = width * twice // lat_count
    split = grads.reshape(kinds * groups, lat_count, piece).transpose(1, 0, 2)
    if kinds * groups * piece % LANES == 0:
        split = split.reshape(lat_count, kinds * groups * piece // LANES, LANES)
    total = jnp.sum(exchange(split), axis=0)
    return total.reshape(kinds, groups, piece)


def with_kernels(field, cotangent, first_weight, first_bias, second_weight, second_bias):
    local_rows, col_count, channels = field.shape
    width = first_weight.shape[1]
    groups = channels // width
    lat_count = lax.axis_size("lat")
    row_count = local_rows * lat_count
    sub_count = KW // lat_count
    waves = zonal_waves(col_count, KW)
    table = (
        waves.reshape(col_count, 2, lat_count, sub_count).transpose(0, 2, 1, 3).reshape(col_count, 2 * KW)
    )
    factor = np.repeat(wave_factor(KW).reshape(lat_count, 1, sub_count), 2, axis=1)
    cosine, sines = meridian_waves(row_count)
    unit = np.eye(PACK, dtype=np.float32)
    mixer = np.concatenate(
        [np.kron(cosine.astype(np.float32), unit), np.kron(sines.astype(np.float32), unit)], axis=1
    ).astype(BF16)
    ahead, back = jnp.asarray(table), jnp.asarray(np.ascontiguousarray(table.T))
    tall_factor = jnp.asarray(factor.reshape(lat_count, 2 * sub_count))
    mixer = jnp.asarray(mixer)
    normalizer = 1.0 / math.sqrt(row_count * KW)
    field, cotangent = field.transpose(0, 2, 1), cotangent.transpose(0, 2, 1)

    arrived = [
        swap_blocks(zonal(field, cotangent, ahead, tall_factor, group, width, lat_count))
        for group in range(groups)
    ]
    returned = [
        swap_blocks(
            middle(
                arrived[group], local_rows, mixer, first_weight, first_bias, second_weight, second_bias,
                group, groups, normalizer,
            )
        )
        for group in range(groups)
    ]
    results = []
    for group in range(groups):
        results = inverse(
            returned[group], back, tall_factor, field, cotangent, group, groups,
            2 * width * width // lat_count, results,
        )
    mixed, field_gradient = (result.transpose(0, 2, 1) for result in results[:2])
    return (mixed, field_gradient, results[2], results[3])


def gelu_value(values):
    tangent = jnp.tanh(GELU_SCALE * (values + GELU_CUBIC * values * values * values))
    return 0.5 * values * (1.0 + tangent)


def gelu_slope(values):
    tangent = jnp.tanh(GELU_SCALE * (values + GELU_CUBIC * values * values * values))
    inner = GELU_SCALE * (1.0 + 3.0 * GELU_CUBIC * values * values)
    return 0.5 * (1.0 + tangent) + 0.5 * values * (1.0 - tangent * tangent) * inner


def contract(pattern, former, latter):
    return jnp.einsum(pattern, former, latter, preferred_element_type=F32)


def complex_block(weights):
    width = weights.shape[1]
    real_part, imag_part = weights[:, :, :width], weights[:, :, width:]
    upper = jnp.stack([real_part, imag_part], axis=2)
    lower = jnp.stack([-imag_part, real_part], axis=2)
    return jnp.stack([upper, lower], axis=1)


def block_gradient(outer):
    real_part = outer[:, 0, :, 0, :] + outer[:, 1, :, 1, :]
    imag_part = outer[:, 0, :, 1, :] - outer[:, 1, :, 0, :]
    return jnp.concatenate([real_part, imag_part], axis=2)


def bias_layout(bias):
    groups, twice = bias.shape
    return bias.reshape(groups, 2, twice // 2).transpose(1, 0, 2)[None, :, None]


def plain(field, cotangent, first_weight, first_bias, second_weight, second_bias):
    local_rows, col_count, channels = field.shape
    width = first_weight.shape[1]
    groups = channels // width
    lat_count = lax.axis_size("lat")
    row_count = local_rows * lat_count
    ahead = jnp.asarray(zonal_waves(col_count, KW))
    factor = jnp.asarray(wave_factor(KW))
    cosine, sines = (jnp.asarray(t) for t in meridian_waves(row_count))
    forth = jnp.stack(
        [jnp.stack([cosine, sines], axis=-1), jnp.stack([-sines, cosine], axis=-1)], axis=1
    )
    first_block = complex_block(local_groups_of(first_weight, groups))
    second_block = complex_block(local_groups_of(second_weight, groups))

    def swap(array, split, concat):
        return lax.all_to_all(array, "lat", split_axis=split, concat_axis=concat, tiled=True)

    spectrum = contract("hwc,wrk->hrkc", field, ahead).astype(BF16)
    adjoint = (contract("hwc,wrk->hrkc", cotangent, ahead) * factor[:, None]).astype(BF16)
    modes, adjoint = swap(spectrum, 2, 0), swap(adjoint, 2, 0)
    block_shape = (row_count, 2, modes.shape[2], groups, width)
    inputs = contract("mphr,hrkc->mpkc", forth, modes).astype(BF16).reshape(block_shape)
    harmonic_adjoint = contract("mphr,hrkc->mpkc", forth, adjoint).reshape(block_shape)
    pre_first = contract("mrkgc,grcsd->mskgd", inputs, first_block) + bias_layout(
        local_groups_of(first_bias, groups)
    )
    hidden = gelu_value(pre_first).astype(BF16)
    pre_second = contract("mrkgc,grcsd->mskgd", hidden, second_block) + bias_layout(
        local_groups_of(second_bias, groups)
    )
    squashed = jnp.tanh(pre_second / SHRINK)
    shrunk = (pre_second - SHRINK * squashed).astype(BF16).reshape(modes.shape)
    second_adjoint = (harmonic_adjoint * (squashed * squashed)).astype(BF16)
    second_grad = block_gradient(contract("mrkgc,mskgd->grcsd", hidden, second_adjoint))
    hidden_adjoint = contract("mskgd,grcsd->mrkgc", second_adjoint, second_block)
    first_adjoint = (hidden_adjoint * gelu_slope(pre_first)).astype(BF16)
    first_grad = block_gradient(contract("mrkgc,mskgd->grcsd", inputs, first_adjoint))
    harmonics_adjoint = contract("mskgd,grcsd->mrkgc", first_adjoint, first_block).astype(BF16)
    synthesis = contract("mphr,mpkc->hrkc", forth, shrunk).astype(BF16)
    returned = contract(
        "mphr,mpkc->hrkc", forth, harmonics_adjoint.reshape(modes.shape)
    ).astype(BF16)
    mixed_modes, return_modes = swap(synthesis, 0, 2), swap(returned, 0, 2)
    gradients = reduce_gradients(
        jnp.stack([first_grad, second_grad]) * (1.0 / math.sqrt(row_count * KW)), lat_count
    )
    mixed_modes = (mixed_modes.astype(F32) * factor[:, None]).astype(BF16)
    mixed = (field.astype(F32) + contract("hrkc,wrk->hwc", mixed_modes, ahead)).astype(BF16)
    field_gradient = (
        cotangent.astype(F32) + contract("hrkc,wrk->hwc", return_modes, ahead)
    ).astype(BF16)
    return (mixed, field_gradient, gradients[0], gradients[1])


def on_device(field, *rest):
    local_rows, _, channels = field.shape
    lat_count = lax.axis_size("lat")
    fits = (
        KW == HALF * lat_count
        and channels == 2 * rest[1].shape[1]
        and local_rows * lat_count % 2 == 0
        and rest[1].shape[1] % (2 * PACK) == 0
        and local_rows * lat_count * PACK <= 512
        and lat_count & (lat_count - 1) == 0
        and rest[1].shape[1] % lat_count == 0
        and rest[1].shape[1] // lat_count <= PACK
        and 2 * rest[1].shape[1] == LANES + HALF
    )
    return (with_kernels if fits else plain)(field, *rest)


def solution(mesh):
    placed = (P(("rep", "lat"), None, "blk"), P(("rep", "lat"), None, "blk"), P(), P(), P(), P())
    return jax.shard_map(
        on_device,
        mesh=mesh,
        in_specs=placed,
        out_specs=(
            P(("rep", "lat"), None, "blk"),
            P(("rep", "lat"), None, "blk"),
            P(("rep", "blk"), "lat"),
            P(("rep", "blk"), "lat"),
        ),
        check_vma=False,
    )
```

```python
import functools
import math

import jax
import jax.numpy as jnp
import numpy as np
from jax import lax
from jax.experimental import pallas as pl
from jax.experimental.pallas import tpu as pltpu
from jax.sharding import PartitionSpec as P

KW = 512
LANES = 128
HALF = 64
PACK = 16
MIB = 1024 * 1024
ZONAL_MIB = 60
MIDDLE_MIB = 24
INVERSE_MIB = 24

SHRINK = 0.01
GELU_SCALE = 0.7978845608028654
GELU_CUBIC = 0.044715
F32 = jnp.float32
BF16 = jnp.bfloat16


def zonal_waves(col_count, kept):
    column = np.arange(col_count, dtype=np.int64)
    wavenumber = np.arange(kept, dtype=np.int64)
    phases = column[:, None] * wavenumber[None, :] % col_count
    angles = phases.astype(np.float32) * np.float32(2.0 * math.pi / col_count)
    scaling = np.float32(1.0 / math.sqrt(col_count))
    cosine = np.cos(angles) * scaling
    sines = np.sin(angles) * scaling
    return np.stack([cosine, -sines], axis=1).astype(BF16)


def meridian_waves(row_count):
    indices = np.arange(row_count, dtype=np.int64)
    phases = indices[:, None] * indices[None, :] % row_count
    angles = phases.astype(np.float32) * np.float32(2.0 * math.pi / row_count)
    scaling = np.float32(1.0 / math.sqrt(row_count))
    return ((np.cos(angles) * scaling).astype(BF16), (np.sin(angles) * scaling).astype(BF16))


def wave_factor(kept):
    return np.where(np.arange(kept) == 0, 1.0, 2.0).astype(np.float32)


def mm(former, latter):
    return jnp.dot(former, latter, preferred_element_type=F32)


def with_swapped(values, first_sign):
    lane = lax.broadcasted_iota(jnp.int32, (1, LANES), 1)
    sign = jnp.where(lane < HALF, first_sign, -first_sign).astype(values.dtype)
    return jnp.concatenate([values, pltpu.roll(values, HALF, axis=1) * sign], axis=0)


def slots(pieces):
    return (0, 7, 1, 6, 2, 5, 3, 4) if pieces == 8 else tuple(range(pieces))


def relative(mine, shift):
    return jnp.bitwise_xor(mine, shift)


def limits(mebibytes):
    return pltpu.CompilerParams(vmem_limit_bytes=mebibytes * MIB)


def zonal_kernel(mine_ref, field_ref, cotangent_ref, table_ref, scale_ref, *rest):
    outs, (rows_ref, pair_ref) = rest[:-2], rest[-2:]
    step = pl.program_id(0)
    lines, width, col_count = field_ref.shape
    half = lines * width

    @pl.when(step == 0)
    def _():
        rows_ref[:half] = field_ref[...].reshape(half, col_count)
        rows_ref[half:] = cotangent_ref[...].reshape(half, col_count)

    odd = jnp.bitwise_and(mine_ref[0], 1)
    result = mm(rows_ref[...], table_ref[0])
    for piece in range(2):
        lanes = slice(piece * LANES, (piece + 1) * LANES)
        pair_ref[piece, :half] = result[:half, lanes].astype(BF16)
        pair_ref[piece, half:] = (result[half:, lanes] * scale_ref[:, lanes]).astype(BF16)
    for place in range(len(outs) // 2):

        @pl.when(step == place)
        def _():
            where = slots(len(outs))
            outs[where.index(2 * place)][...] = pair_ref[odd]
            outs[where.index(2 * place + 1)][...] = pair_ref[1 - odd]


def zonal(mine, field, cotangent, table, scale, group, width, pieces):
    lines, _, col_count = field.shape
    rows = 2 * lines * width
    wide = 2 * LANES

    def block_of(i, place):
        return jnp.bitwise_xor(lax.shift_right_logical(place[0], 1), i)

    own = pl.BlockSpec((lines, width, col_count), lambda i, place: (0, group, 0))
    return pl.pallas_call(
        zonal_kernel,
        grid_spec=pltpu.PrefetchScalarGridSpec(
            num_scalar_prefetch=1,
            grid=(pieces // 2,),
            in_specs=[
                own,
                own,
                pl.BlockSpec((1, col_count, wide), lambda i, place: (block_of(i, place), 0, 0)),
                pl.BlockSpec((1, wide), lambda i, place: (0, block_of(i, place))),
            ],
            out_specs=[pl.BlockSpec((rows, LANES), lambda i, place: (0, 0)) for _ in range(pieces)],
            scratch_shapes=[pltpu.VMEM((rows, col_count), BF16), pltpu.VMEM((2, rows, LANES), BF16)],
        ),
        out_shape=[jax.ShapeDtypeStruct((rows, LANES), BF16) for _ in range(pieces)],
        compiler_params=limits(ZONAL_MIB if group == 0 else MIDDLE_MIB),
        cost_estimate=pl.CostEstimate(flops=4 * 10**9, bytes_accessed=4 * MIB, transcendentals=0),
    )(mine, field, cotangent, table, scale)


def inverse_kernel(pieces, given, group, *refs):
    blocks = refs[:pieces]
    table_ref, scale_ref, field_ref, cotangent_ref = refs[pieces : pieces + 4]
    before = refs[pieces + 4 : pieces + 4 + given]
    mixed_ref, gradient_ref, first_ref, second_ref, modes_ref = refs[pieces + 4 + given :]
    rows = modes_ref.shape[1]
    half = rows // 2

    @pl.when(pl.program_id(0) == 0)
    def _():
        mine = lax.axis_index("lat")
        for block, shift in zip(blocks, slots(pieces)):
            place = relative(mine, shift)
            scale = scale_ref[pl.ds(place, 1), :]
            modes_ref[place, :half] = (block[:half].astype(F32) * scale).astype(BF16)
            modes_ref[place, half:] = block[half:rows]
        total = blocks[0][rows:].astype(F32)
        for block in blocks[1:]:
            total += block[rows:].astype(F32)
        spread_gradient(total, 0, group, before[2:3], first_ref)
        spread_gradient(total, 1, group, before[3:4], second_ref)

    modes = jnp.concatenate([modes_ref[piece] for piece in range(pieces)], axis=1)
    result = mm(modes, table_ref[...])
    shape = field_ref.shape
    mixed_ref[...] = (field_ref[...].astype(F32) + result[:half].reshape(shape)).astype(BF16)
    gradient_ref[...] = (cotangent_ref[...].astype(F32) + result[half:].reshape(shape)).astype(BF16)


def spread_gradient(total, kind, group, before, out_ref):
    for member in range(group):
        out_ref[member : member + 1] = before[0][member : member + 1]
    lines = []
    for line in range(out_ref.shape[1] // (LANES + HALF)):
        lines.append(total[kind * PACK + line : kind * PACK + line + 1])
        lines.append(total[2 * PACK + line : 2 * PACK + line + 1, kind * HALF : (kind + 1) * HALF])
    out_ref[group : group + 1] = jnp.concatenate(lines, axis=1)


def pack_gradients(sums_ref, packed_ref):
    pieces = packed_ref.shape[0]
    part = (sums_ref.shape[1] - PACK) // pieces
    for piece in range(pieces):
        lines = slice(piece * part, piece * part + PACK)
        both = [sums_ref[kind, lines, :] for kind in range(2)]
        for kind in range(2):
            packed_ref[piece, kind * PACK : (kind + 1) * PACK] = both[kind][:, :LANES].astype(BF16)
        tails = jnp.concatenate([value[:, LANES:] for value in both], axis=1)
        packed_ref[piece, 2 * PACK :] = tails.astype(BF16)


def inverse(blocks, table, scale, field, cotangent, group, groups, gradient_size, before):
    pieces = len(blocks)
    kept, col_count = table.shape
    lines, channels, _ = field.shape
    width = channels // groups
    rows = 2 * lines * width
    wide = 512
    own = pl.BlockSpec((lines, width, wide), lambda i: (0, group, i))
    anywhere = pl.BlockSpec(memory_space=pl.ANY)
    gradient = pl.BlockSpec((groups, gradient_size), lambda i: (0, 0))
    return pl.pallas_call(
        functools.partial(inverse_kernel, pieces, len(before), group),
        grid=(pl.cdiv(col_count, wide),),
        in_specs=[pl.BlockSpec(block.shape, lambda i: (0, 0)) for block in blocks]
        + [
            pl.BlockSpec((kept, wide), lambda i: (0, i)),
            pl.BlockSpec(scale.shape, lambda i: (0, 0)),
            own,
            own,
        ]
        + ([anywhere, anywhere, gradient, gradient] if before else []),
        out_specs=[own, own, gradient, gradient],
        out_shape=[jax.ShapeDtypeStruct(field.shape, BF16) for _ in range(2)]
        + [jax.ShapeDtypeStruct((groups, gradient_size), F32) for _ in range(2)],
        scratch_shapes=[pltpu.VMEM((pieces, rows, LANES), BF16)],
        input_output_aliases={pieces + 4 + i: i for i in range(2)} if before else {},
        compiler_params=limits(INVERSE_MIB),
        cost_estimate=pl.CostEstimate(flops=4 * 10**9, bytes_accessed=5 * MIB, transcendentals=0),
    )(*blocks, table, scale, field, cotangent, *before)


def meridian(load, mixer, first_sign, channels, store):
    count = mixer.shape[0] // PACK
    for start in range(0, channels, 2 * PACK):
        pair = [
            with_swapped(load(start + shift).reshape(count * PACK, LANES), first_sign)
            for shift in (0, PACK)
        ]
        both = mm(mixer[...], side_by_side(pair))
        for index in range(2):
            value = both[:, index * LANES : (index + 1) * LANES]
            store(start + index * PACK, value.reshape(count, PACK, LANES))


def nt(former, latter):
    return lax.dot_general(former, latter, (((1,), (1,)), ((), ())), preferred_element_type=F32)


def side_by_side(pieces):
    return jnp.concatenate(pieces, axis=1)


def bias_lanes(bias_ref, index):
    tall = jnp.broadcast_to(bias_ref[pl.ds(index, 1), :], (LANES, bias_ref.shape[1])).T
    width = bias_ref.shape[1] // 2
    lane = lax.broadcasted_iota(jnp.int32, (1, LANES), 1)
    return jnp.where(lane < HALF, tall[:width], tall[width:])


def forth(weight):
    width = weight.shape[0]
    turned = weight.T
    return side_by_side([turned[:width], turned[width:]])


def middle_kernel(group, groups, normalizer, pieces, *refs):
    blocks, refs = refs[:pieces], refs[pieces:]
    (mixer_ref, first_ref, first_bias_ref, second_ref, second_bias_ref), refs = refs[:5], refs[5:]
    outs, refs = refs[:pieces], refs[pieces:]
    modes_ref, adjoint_ref, harm_ref, shrunk_ref, exact_ref, sums_ref, packed_ref = refs
    mine = lax.axis_index("lat")
    index = lax.axis_index("blk") * groups + group
    count, width, _ = modes_ref.shape
    lines = count // pieces
    for block, shift in zip(blocks, slots(pieces)):
        for line in range(lines):
            row = relative(mine, shift) * lines + line
            modes_ref[row] = block[line * width : (line + 1) * width]
            adjoint_ref[row] = block[(lines + line) * width : (lines + line + 1) * width]

    first, second = first_ref[index], second_ref[index]
    first_ahead, second_ahead = forth(first), forth(second)
    first_bias, second_bias = bias_lanes(first_bias_ref, index), bias_lanes(second_bias_ref, index)

    def keep(start, value):
        harm_ref[:, start : start + PACK, :] = value.astype(BF16)

    meridian(lambda c: modes_ref[:, c : c + PACK, :], mixer_ref, 1.0, width, keep)

    def keep_adjoint(start, value):
        exact_ref[:, start : start + PACK, :] = value

    meridian(lambda c: adjoint_ref[:, c : c + PACK, :], mixer_ref, 1.0, width, keep_adjoint)

    first_sum = jnp.zeros((width, 2 * width), F32)
    second_sum = jnp.zeros((width, 2 * width), F32)
    step = 4
    for row in range(0, count, step):
        members = range(step)

        def lanes_of(wide):
            return [wide[:, i * LANES : (i + 1) * LANES] for i in members]

        inputs = [harm_ref[row + i] for i in members]
        pre = lanes_of(mm(first_ahead, side_by_side([with_swapped(x, -1.0) for x in inputs])))
        hidden, slope = [], []
        for i in members:
            v = pre[i] + first_bias
            square = v * v
            tangent = jnp.tanh(v * (GELU_SCALE + GELU_SCALE * GELU_CUBIC * square))
            outer = 0.5 + 0.5 * tangent
            inner = 0.5 * GELU_SCALE + 1.5 * GELU_SCALE * GELU_CUBIC * square
            hidden.append((v * outer).astype(BF16))
            slope.append(outer + v * (1.0 - tangent * tangent) * inner)
        pre = lanes_of(mm(second_ahead, side_by_side([with_swapped(x, -1.0) for x in hidden])))
        second_adjoint = []
        for i in members:
            v = pre[i] + second_bias
            squashed = jnp.tanh(v * (1.0 / SHRINK))
            shrunk_ref[row + i] = (v - SHRINK * squashed).astype(BF16)
            second_adjoint.append((exact_ref[row + i] * (squashed * squashed)).astype(BF16))
        pairs = side_by_side([with_swapped(x, 1.0) for x in second_adjoint])
        second_sum += nt(side_by_side(hidden), pairs)
        back = lanes_of(mm(second, pairs))
        first_adjoint = [(back[i] * slope[i]).astype(BF16) for i in members]
        pairs = side_by_side([with_swapped(x, 1.0) for x in first_adjoint])
        first_sum += nt(side_by_side(inputs), pairs)
        back = lanes_of(mm(first, pairs))
        for i in members:
            harm_ref[row + i] = back[i].astype(BF16)

    sums_ref[0, :width] = first_sum * normalizer
    sums_ref[1, :width] = second_sum * normalizer
    sums_ref[:, width:] = jnp.zeros((2, PACK, 2 * width), F32)
    pack_gradients(sums_ref, packed_ref)

    def emit(start, value):
        modes_ref[:, start : start + PACK, :] = value.astype(BF16)

    def emit_adjoint(start, value):
        adjoint_ref[:, start : start + PACK, :] = value.astype(BF16)

    meridian(lambda c: shrunk_ref[:, c : c + PACK, :], mixer_ref, -1.0, width, emit)
    meridian(lambda c: harm_ref[:, c : c + PACK, :], mixer_ref, -1.0, width, emit_adjoint)
    for out, shift in zip(outs, slots(pieces)):
        for line in range(lines):
            row = relative(mine, shift) * lines + line
            out[line * width : (line + 1) * width] = modes_ref[row]
            out[(lines + line) * width : (lines + line + 1) * width] = adjoint_ref[row]
        out[2 * lines * width :] = packed_ref[relative(mine, shift)]


def whole(*shape):
    return pl.BlockSpec(shape, lambda: (0,) * len(shape))


def middle(blocks, lines, mixer, first, first_bias, second, second_bias, group, groups, normalizer):
    pieces = len(blocks)
    width = first.shape[1]
    shape = (pieces * lines, width, LANES)
    operands = (*blocks, mixer, first, first_bias, second, second_bias)
    longer = (blocks[0].shape[0] + 3 * PACK, LANES)
    return pl.pallas_call(
        functools.partial(middle_kernel, group, groups, normalizer, pieces),
        in_specs=[whole(*a.shape) for a in operands],
        out_specs=[whole(*longer) for _ in blocks],
        out_shape=[jax.ShapeDtypeStruct(longer, BF16) for _ in blocks],
        scratch_shapes=[pltpu.VMEM(shape, BF16) for _ in range(4)]
        + [
            pltpu.VMEM(shape, F32),
            pltpu.VMEM((2, width + PACK, 2 * width), F32),
            pltpu.VMEM((pieces, 3 * PACK, LANES), BF16),
        ],
        compiler_params=limits(MIDDLE_MIB),
        cost_estimate=pl.CostEstimate(flops=7 * 10**9, bytes_accessed=4 * MIB, transcendentals=0),
    )(*operands)


def local_groups_of(array, groups):
    return lax.dynamic_slice_in_dim(array, lax.axis_index("blk") * groups, groups, axis=0)


def exchange(blocks):
    return lax.all_to_all(blocks, "lat", split_axis=0, concat_axis=0, tiled=True)


def pass_to(block, shift):
    count = lax.axis_size("lat")
    return lax.ppermute(block, "lat", [(place, place ^ shift) for place in range(count)])


def swap_blocks(blocks):
    return [pass_to(block, shift) if shift else block for block, shift in zip(blocks, slots(len(blocks)))]


def reduce_gradients(grads, lat_count):
    kinds, groups, width, twice = grads.shape
    piece = width * twice // lat_count
    split = grads.reshape(kinds * groups, lat_count, piece).transpose(1, 0, 2)
    if kinds * groups * piece % LANES == 0:
        split = split.reshape(lat_count, kinds * groups * piece // LANES, LANES)
    total = jnp.sum(exchange(split), axis=0)
    return total.reshape(kinds, groups, piece)


def with_kernels(field, cotangent, first_weight, first_bias, second_weight, second_bias):
    local_rows, col_count, channels = field.shape
    width = first_weight.shape[1]
    groups = channels // width
    lat_count = lax.axis_size("lat")
    row_count = local_rows * lat_count
    sub_count = KW // lat_count
    waves = zonal_waves(col_count, KW)
    table = (
        waves.reshape(col_count, 2, lat_count, sub_count).transpose(0, 2, 1, 3).reshape(col_count, 2 * KW)
    )
    factor = np.repeat(wave_factor(KW).reshape(lat_count, 1, sub_count), 2, axis=1)
    cosine, sines = meridian_waves(row_count)
    unit = np.eye(PACK, dtype=np.float32)
    mixer = np.concatenate(
        [np.kron(cosine.astype(np.float32), unit), np.kron(sines.astype(np.float32), unit)], axis=1
    ).astype(BF16)
    chunks = table.reshape(col_count, lat_count // 2, 2 * LANES).transpose(1, 0, 2)
    ahead, back = jnp.asarray(np.ascontiguousarray(chunks)), jnp.asarray(np.ascontiguousarray(table.T))
    wide_factor = jnp.asarray(factor.reshape(1, 2 * KW))
    tall_factor = jnp.asarray(factor.reshape(lat_count, 2 * sub_count))
    mixer = jnp.asarray(mixer)
    normalizer = 1.0 / math.sqrt(row_count * KW)
    mine = lax.axis_index("lat").astype(jnp.int32).reshape(1)
    field, cotangent = field.transpose(0, 2, 1), cotangent.transpose(0, 2, 1)

    arrived = [
        swap_blocks(zonal(mine, field, cotangent, ahead, wide_factor, group, width, lat_count))
        for group in range(groups)
    ]
    returned = [
        swap_blocks(
            middle(
                arrived[group], local_rows, mixer, first_weight, first_bias, second_weight, second_bias,
                group, groups, normalizer,
            )
        )
        for group in range(groups)
    ]
    results = []
    for group in range(groups):
        results = inverse(
            returned[group], back, tall_factor, field, cotangent, group, groups,
            2 * width * width // lat_count, results,
        )
    mixed, field_gradient = (result.transpose(0, 2, 1) for result in results[:2])
    return (mixed, field_gradient, results[2], results[3])


def gelu_value(values):
    tangent = jnp.tanh(GELU_SCALE * (values + GELU_CUBIC * values * values * values))
    return 0.5 * values * (1.0 + tangent)


def gelu_slope(values):
    tangent = jnp.tanh(GELU_SCALE * (values + GELU_CUBIC * values * values * values))
    inner = GELU_SCALE * (1.0 + 3.0 * GELU_CUBIC * values * values)
    return 0.5 * (1.0 + tangent) + 0.5 * values * (1.0 - tangent * tangent) * inner


def contract(pattern, former, latter):
    return jnp.einsum(pattern, former, latter, preferred_element_type=F32)


def complex_block(weights):
    width = weights.shape[1]
    real_part, imag_part = weights[:, :, :width], weights[:, :, width:]
    upper = jnp.stack([real_part, imag_part], axis=2)
    lower = jnp.stack([-imag_part, real_part], axis=2)
    return jnp.stack([upper, lower], axis=1)


def block_gradient(outer):
    real_part = outer[:, 0, :, 0, :] + outer[:, 1, :, 1, :]
    imag_part = outer[:, 0, :, 1, :] - outer[:, 1, :, 0, :]
    return jnp.concatenate([real_part, imag_part], axis=2)


def bias_layout(bias):
    groups, twice = bias.shape
    return bias.reshape(groups, 2, twice // 2).transpose(1, 0, 2)[None, :, None]


def plain(field, cotangent, first_weight, first_bias, second_weight, second_bias):
    local_rows, col_count, channels = field.shape
    width = first_weight.shape[1]
    groups = channels // width
    lat_count = lax.axis_size("lat")
    row_count = local_rows * lat_count
    ahead = jnp.asarray(zonal_waves(col_count, KW))
    factor = jnp.asarray(wave_factor(KW))
    cosine, sines = (jnp.asarray(t) for t in meridian_waves(row_count))
    forth = jnp.stack(
        [jnp.stack([cosine, sines], axis=-1), jnp.stack([-sines, cosine], axis=-1)], axis=1
    )
    first_block = complex_block(local_groups_of(first_weight, groups))
    second_block = complex_block(local_groups_of(second_weight, groups))

    def swap(array, split, concat):
        return lax.all_to_all(array, "lat", split_axis=split, concat_axis=concat, tiled=True)

    spectrum = contract("hwc,wrk->hrkc", field, ahead).astype(BF16)
    adjoint = (contract("hwc,wrk->hrkc", cotangent, ahead) * factor[:, None]).astype(BF16)
    modes, adjoint = swap(spectrum, 2, 0), swap(adjoint, 2, 0)
    block_shape = (row_count, 2, modes.shape[2], groups, width)
    inputs = contract("mphr,hrkc->mpkc", forth, modes).astype(BF16).reshape(block_shape)
    harmonic_adjoint = contract("mphr,hrkc->mpkc", forth, adjoint).reshape(block_shape)
    pre_first = contract("mrkgc,grcsd->mskgd", inputs, first_block) + bias_layout(
        local_groups_of(first_bias, groups)
    )
    hidden = gelu_value(pre_first).astype(BF16)
    pre_second = contract("mrkgc,grcsd->mskgd", hidden, second_block) + bias_layout(
        local_groups_of(second_bias, groups)
    )
    squashed = jnp.tanh(pre_second / SHRINK)
    shrunk = (pre_second - SHRINK * squashed).astype(BF16).reshape(modes.shape)
    second_adjoint = (harmonic_adjoint * (squashed * squashed)).astype(BF16)
    second_grad = block_gradient(contract("mrkgc,mskgd->grcsd", hidden, second_adjoint))
    hidden_adjoint = contract("mskgd,grcsd->mrkgc", second_adjoint, second_block)
    first_adjoint = (hidden_adjoint * gelu_slope(pre_first)).astype(BF16)
    first_grad = block_gradient(contract("mrkgc,mskgd->grcsd", inputs, first_adjoint))
    harmonics_adjoint = contract("mskgd,grcsd->mrkgc", first_adjoint, first_block).astype(BF16)
    synthesis = contract("mphr,mpkc->hrkc", forth, shrunk).astype(BF16)
    returned = contract(
        "mphr,mpkc->hrkc", forth, harmonics_adjoint.reshape(modes.shape)
    ).astype(BF16)
    mixed_modes, return_modes = swap(synthesis, 0, 2), swap(returned, 0, 2)
    gradients = reduce_gradients(
        jnp.stack([first_grad, second_grad]) * (1.0 / math.sqrt(row_count * KW)), lat_count
    )
    mixed_modes = (mixed_modes.astype(F32) * factor[:, None]).astype(BF16)
    mixed = (field.astype(F32) + contract("hrkc,wrk->hwc", mixed_modes, ahead)).astype(BF16)
    field_gradient = (
        cotangent.astype(F32) + contract("hrkc,wrk->hwc", return_modes, ahead)
    ).astype(BF16)
    return (mixed, field_gradient, gradients[0], gradients[1])


def on_device(field, *rest):
    local_rows, _, channels = field.shape
    lat_count = lax.axis_size("lat")
    fits = (
        KW == HALF * lat_count
        and channels == 2 * rest[1].shape[1]
        and local_rows * lat_count % 2 == 0
        and rest[1].shape[1] % (2 * PACK) == 0
        and local_rows * lat_count * PACK <= 512
        and lat_count & (lat_count - 1) == 0
        and rest[1].shape[1] % lat_count == 0
        and rest[1].shape[1] // lat_count <= PACK
        and 2 * rest[1].shape[1] == LANES + HALF
    )
    return (with_kernels if fits else plain)(field, *rest)


def solution(mesh):
    placed = (P(("rep", "lat"), None, "blk"), P(("rep", "lat"), None, "blk"), P(), P(), P(), P())
    return jax.shard_map(
        on_device,
        mesh=mesh,
        in_specs=placed,
        out_specs=(
            P(("rep", "lat"), None, "blk"),
            P(("rep", "lat"), None, "blk"),
            P(("rep", "blk"), "lat"),
            P(("rep", "blk"), "lat"),
        ),
        check_vma=False,
    )
```

```python
import functools
import math

import jax
import jax.numpy as jnp
import numpy as np
from jax import lax
from jax.experimental import pallas as pl
from jax.experimental.pallas import tpu as pltpu
from jax.sharding import PartitionSpec as P

KW = 512
LANES = 128
HALF = 64
CHUNK = 512
PACK = 16
MIB = 1024 * 1024
ZONAL_MIB = 60
MIDDLE_MIB = 24
INVERSE_MIB = 24

SHRINK = 0.01
GELU_SCALE = 0.7978845608028654
GELU_CUBIC = 0.044715
F32 = jnp.float32
BF16 = jnp.bfloat16


def zonal_waves(col_count, kept):
    column = np.arange(col_count, dtype=np.int64)
    wavenumber = np.arange(kept, dtype=np.int64)
    phases = column[:, None] * wavenumber[None, :] % col_count
    angles = phases.astype(np.float32) * np.float32(2.0 * math.pi / col_count)
    scaling = np.float32(1.0 / math.sqrt(col_count))
    cosine = np.cos(angles) * scaling
    sines = np.sin(angles) * scaling
    return np.stack([cosine, -sines], axis=1).astype(BF16)


def meridian_waves(row_count):
    indices = np.arange(row_count, dtype=np.int64)
    phases = indices[:, None] * indices[None, :] % row_count
    angles = phases.astype(np.float32) * np.float32(2.0 * math.pi / row_count)
    scaling = np.float32(1.0 / math.sqrt(row_count))
    return ((np.cos(angles) * scaling).astype(BF16), (np.sin(angles) * scaling).astype(BF16))


def wave_factor(kept):
    return np.where(np.arange(kept) == 0, 1.0, 2.0).astype(np.float32)


def mm(former, latter):
    return jnp.dot(former, latter, preferred_element_type=F32)


def with_swapped(values, first_sign):
    lane = lax.broadcasted_iota(jnp.int32, (1, LANES), 1)
    sign = jnp.where(lane < HALF, first_sign, -first_sign).astype(values.dtype)
    return jnp.concatenate([values, pltpu.roll(values, HALF, axis=1) * sign], axis=0)


def slots(pieces):
    return (0, 7, 1, 6, 2, 5, 3, 4) if pieces == 8 else tuple(range(pieces))


def relative(mine, shift):
    return jnp.bitwise_xor(mine, shift)


def limits(mebibytes):
    return pltpu.CompilerParams(vmem_limit_bytes=mebibytes * MIB)


def zonal_kernel(mine_ref, field_ref, cotangent_ref, table_ref, scale_ref, *rest):
    outs, (rows_ref, pair_ref) = rest[:-2], rest[-2:]
    step = pl.program_id(0)
    lines, width, col_count = field_ref.shape
    half = lines * width

    @pl.when(step == 0)
    def _():
        rows_ref[:half] = field_ref[...].reshape(half, col_count)
        rows_ref[half:] = cotangent_ref[...].reshape(half, col_count)

    odd = jnp.bitwise_and(mine_ref[0], 1)
    result = mm(rows_ref[...], table_ref[0])
    for piece in range(2):
        lanes = slice(piece * LANES, (piece + 1) * LANES)
        pair_ref[piece, :half] = result[:half, lanes].astype(BF16)
        pair_ref[piece, half:] = (result[half:, lanes] * scale_ref[:, lanes]).astype(BF16)
    for place in range(len(outs) // 2):

        @pl.when(step == place)
        def _():
            where = slots(len(outs))
            outs[where.index(2 * place)][...] = pair_ref[odd]
            outs[where.index(2 * place + 1)][...] = pair_ref[1 - odd]


def zonal(mine, field, cotangent, table, scale, group, width, pieces):
    lines, _, col_count = field.shape
    rows = 2 * lines * width
    wide = 2 * LANES

    def block_of(i, place):
        return jnp.bitwise_xor(lax.shift_right_logical(place[0], 1), i)

    own = pl.BlockSpec((lines, width, col_count), lambda i, place: (0, group, 0))
    return pl.pallas_call(
        zonal_kernel,
        grid_spec=pltpu.PrefetchScalarGridSpec(
            num_scalar_prefetch=1,
            grid=(pieces // 2,),
            in_specs=[
                own,
                own,
                pl.BlockSpec((1, col_count, wide), lambda i, place: (block_of(i, place), 0, 0)),
                pl.BlockSpec((1, wide), lambda i, place: (0, block_of(i, place))),
            ],
            out_specs=[pl.BlockSpec((rows, LANES), lambda i, place: (0, 0)) for _ in range(pieces)],
            scratch_shapes=[pltpu.VMEM((rows, col_count), BF16), pltpu.VMEM((2, rows, LANES), BF16)],
        ),
        out_shape=[jax.ShapeDtypeStruct((rows, LANES), BF16) for _ in range(pieces)],
        compiler_params=limits(ZONAL_MIB if group == 0 else MIDDLE_MIB),
        cost_estimate=pl.CostEstimate(flops=4 * 10**9, bytes_accessed=4 * MIB, transcendentals=0),
    )(mine, field, cotangent, table, scale)


def inverse_kernel(pieces, given, group, *refs):
    blocks = refs[:pieces]
    table_ref, scale_ref, field_ref, cotangent_ref = refs[pieces : pieces + 4]
    before = refs[pieces + 4 : pieces + 4 + given]
    mixed_ref, gradient_ref, first_ref, second_ref = refs[pieces + 4 + given : pieces + 8 + given]
    modes_ref, results_ref, flat_ref, sems, flat_sems = refs[pieces + 8 + given :]
    rows = modes_ref.shape[1]
    half = rows // 2
    _, lines, width, col_count = results_ref.shape
    own = slice(group * width, (group + 1) * width)
    mine = lax.axis_index("lat")
    for block, shift in zip(blocks, slots(pieces)):
        place = relative(mine, shift)
        scale = scale_ref[pl.ds(place, 1), :]
        modes_ref[place, :half] = (block[:half].astype(F32) * scale).astype(BF16)
        modes_ref[place, half:] = block[half:rows]

    modes = jnp.concatenate([modes_ref[piece] for piece in range(pieces)], axis=1)
    copies = []
    for chunk, begin in enumerate(range(0, col_count, CHUNK)):
        columns = slice(begin, min(begin + CHUNK, col_count))
        result = mm(modes, table_ref[:, columns])
        for kind, (base, out) in enumerate(((field_ref, mixed_ref), (cotangent_ref, gradient_ref))):
            part = result[kind * half : (kind + 1) * half].reshape(lines, width, -1)
            results_ref[kind, :, :, columns] = (base[:, own, columns].astype(F32) + part).astype(BF16)
            copy = pltpu.make_async_copy(
                results_ref.at[kind, :, :, columns], out.at[:, own, columns], sems.at[chunk, kind]
            )
            copy.start()
            copies.append(copy)
        if begin == 0:
            total = blocks[0][rows:].astype(F32)
            for block in blocks[1:]:
                total += block[rows:].astype(F32)
            for kind, out in enumerate((first_ref, second_ref)):
                spread_gradient(total, kind, group, before[2 + kind : 3 + kind], flat_ref.at[kind])
                copy = pltpu.make_async_copy(flat_ref.at[kind], out, flat_sems.at[kind])
                copy.start()
                copies.append(copy)

    for copy in copies:
        copy.wait()


def spread_gradient(total, kind, group, before, out_ref):
    for member in range(group):
        out_ref[member : member + 1] = before[0][member : member + 1]
    lines = []
    for line in range(out_ref.shape[1] // (LANES + HALF)):
        lines.append(total[kind * PACK + line : kind * PACK + line + 1])
        lines.append(total[2 * PACK + line : 2 * PACK + line + 1, kind * HALF : (kind + 1) * HALF])
    out_ref[group : group + 1] = jnp.concatenate(lines, axis=1)
    for member in range(group + 1, out_ref.shape[0]):
        out_ref[member : member + 1] = jnp.zeros((1, out_ref.shape[1]), F32)


def pack_gradients(sums_ref, packed_ref):
    pieces = packed_ref.shape[0]
    part = (sums_ref.shape[1] - PACK) // pieces
    for piece in range(pieces):
        lines = slice(piece * part, piece * part + PACK)
        both = [sums_ref[kind, lines, :] for kind in range(2)]
        for kind in range(2):
            packed_ref[piece, kind * PACK : (kind + 1) * PACK] = both[kind][:, :LANES].astype(BF16)
        tails = jnp.concatenate([value[:, LANES:] for value in both], axis=1)
        packed_ref[piece, 2 * PACK :] = tails.astype(BF16)


def inverse(blocks, table, scale, field, cotangent, group, groups, gradient_size, before):
    pieces = len(blocks)
    lines, channels, col_count = field.shape
    width = channels // groups
    anywhere = pl.BlockSpec(memory_space=pl.ANY)
    gradient = whole(groups, gradient_size)
    return pl.pallas_call(
        functools.partial(inverse_kernel, pieces, len(before), group),
        in_specs=[whole(*a.shape) for a in (*blocks, table, scale, field, cotangent)]
        + ([anywhere, anywhere, gradient, gradient] if before else []),
        out_specs=[anywhere] * 4,
        out_shape=[jax.ShapeDtypeStruct(field.shape, BF16) for _ in range(2)]
        + [jax.ShapeDtypeStruct((groups, gradient_size), F32) for _ in range(2)],
        scratch_shapes=[
            pltpu.VMEM((pieces, 2 * lines * width, LANES), BF16),
            pltpu.VMEM((2, lines, width, col_count), BF16),
            pltpu.VMEM((2, groups, gradient_size), F32),
            pltpu.SemaphoreType.DMA((pl.cdiv(col_count, CHUNK), 2)),
            pltpu.SemaphoreType.DMA((2,)),
        ],
        input_output_aliases={pieces + 4 + i: i for i in range(2)} if before else {},
        compiler_params=limits(INVERSE_MIB),
        cost_estimate=pl.CostEstimate(flops=4 * 10**9, bytes_accessed=5 * MIB, transcendentals=0),
    )(*blocks, table, scale, field, cotangent, *before)


def meridian(load, mixer, first_sign, channels, store):
    count = mixer.shape[0] // PACK
    for start in range(0, channels, 2 * PACK):
        pair = [
            with_swapped(load(start + shift).reshape(count * PACK, LANES), first_sign)
            for shift in (0, PACK)
        ]
        both = mm(mixer[...], side_by_side(pair))
        for index in range(2):
            value = both[:, index * LANES : (index + 1) * LANES]
            store(start + index * PACK, value.reshape(count, PACK, LANES))


def nt(former, latter):
    return lax.dot_general(former, latter, (((1,), (1,)), ((), ())), preferred_element_type=F32)


def side_by_side(pieces):
    return jnp.concatenate(pieces, axis=1)


def bias_lanes(bias_ref, index):
    tall = jnp.broadcast_to(bias_ref[pl.ds(index, 1), :], (LANES, bias_ref.shape[1])).T
    width = bias_ref.shape[1] // 2
    lane = lax.broadcasted_iota(jnp.int32, (1, LANES), 1)
    return jnp.where(lane < HALF, tall[:width], tall[width:])


def forth(weight):
    width = weight.shape[0]
    turned = weight.T
    return side_by_side([turned[:width], turned[width:]])


def middle_kernel(group, groups, normalizer, pieces, *refs):
    blocks, refs = refs[:pieces], refs[pieces:]
    (mixer_ref, first_ref, first_bias_ref, second_ref, second_bias_ref), refs = refs[:5], refs[5:]
    outs, refs = refs[:pieces], refs[pieces:]
    modes_ref, adjoint_ref, harm_ref, shrunk_ref, exact_ref, sums_ref, packed_ref = refs
    mine = lax.axis_index("lat")
    index = lax.axis_index("blk") * groups + group
    count, width, _ = modes_ref.shape
    lines = count // pieces
    for block, shift in zip(blocks, slots(pieces)):
        for line in range(lines):
            row = relative(mine, shift) * lines + line
            modes_ref[row] = block[line * width : (line + 1) * width]
            adjoint_ref[row] = block[(lines + line) * width : (lines + line + 1) * width]

    first, second = first_ref[index], second_ref[index]
    first_ahead, second_ahead = forth(first), forth(second)
    first_bias, second_bias = bias_lanes(first_bias_ref, index), bias_lanes(second_bias_ref, index)

    def keep(start, value):
        harm_ref[:, start : start + PACK, :] = value.astype(BF16)

    meridian(lambda c: modes_ref[:, c : c + PACK, :], mixer_ref, 1.0, width, keep)

    def keep_adjoint(start, value):
        exact_ref[:, start : start + PACK, :] = value

    meridian(lambda c: adjoint_ref[:, c : c + PACK, :], mixer_ref, 1.0, width, keep_adjoint)

    first_sum = jnp.zeros((width, 2 * width), F32)
    second_sum = jnp.zeros((width, 2 * width), F32)
    step = 4
    for row in range(0, count, step):
        members = range(step)

        def lanes_of(wide):
            return [wide[:, i * LANES : (i + 1) * LANES] for i in members]

        inputs = [harm_ref[row + i] for i in members]
        pre = lanes_of(mm(first_ahead, side_by_side([with_swapped(x, -1.0) for x in inputs])))
        hidden, slope = [], []
        for i in members:
            v = pre[i] + first_bias
            square = v * v
            tangent = jnp.tanh(v * (GELU_SCALE + GELU_SCALE * GELU_CUBIC * square))
            outer = 0.5 + 0.5 * tangent
            inner = 0.5 * GELU_SCALE + 1.5 * GELU_SCALE * GELU_CUBIC * square
            hidden.append((v * outer).astype(BF16))
            slope.append(outer + v * (1.0 - tangent * tangent) * inner)
        pre = lanes_of(mm(second_ahead, side_by_side([with_swapped(x, -1.0) for x in hidden])))
        second_adjoint = []
        for i in members:
            v = pre[i] + second_bias
            squashed = jnp.tanh(v * (1.0 / SHRINK))
            shrunk_ref[row + i] = (v - SHRINK * squashed).astype(BF16)
            second_adjoint.append((exact_ref[row + i] * (squashed * squashed)).astype(BF16))
        pairs = side_by_side([with_swapped(x, 1.0) for x in second_adjoint])
        second_sum += nt(side_by_side(hidden), pairs)
        back = lanes_of(mm(second, pairs))
        first_adjoint = [(back[i] * slope[i]).astype(BF16) for i in members]
        pairs = side_by_side([with_swapped(x, 1.0) for x in first_adjoint])
        first_sum += nt(side_by_side(inputs), pairs)
        back = lanes_of(mm(first, pairs))
        for i in members:
            harm_ref[row + i] = back[i].astype(BF16)

    sums_ref[0, :width] = first_sum * normalizer
    sums_ref[1, :width] = second_sum * normalizer
    sums_ref[:, width:] = jnp.zeros((2, PACK, 2 * width), F32)
    pack_gradients(sums_ref, packed_ref)

    def emit(start, value):
        modes_ref[:, start : start + PACK, :] = value.astype(BF16)

    def emit_adjoint(start, value):
        adjoint_ref[:, start : start + PACK, :] = value.astype(BF16)

    meridian(lambda c: shrunk_ref[:, c : c + PACK, :], mixer_ref, -1.0, width, emit)
    meridian(lambda c: harm_ref[:, c : c + PACK, :], mixer_ref, -1.0, width, emit_adjoint)
    for out, shift in zip(outs, slots(pieces)):
        for line in range(lines):
            row = relative(mine, shift) * lines + line
            out[line * width : (line + 1) * width] = modes_ref[row]
            out[(lines + line) * width : (lines + line + 1) * width] = adjoint_ref[row]
        out[2 * lines * width :] = packed_ref[relative(mine, shift)]


def whole(*shape):
    return pl.BlockSpec(shape, lambda: (0,) * len(shape))


def middle(blocks, lines, mixer, first, first_bias, second, second_bias, group, groups, normalizer):
    pieces = len(blocks)
    width = first.shape[1]
    shape = (pieces * lines, width, LANES)
    operands = (*blocks, mixer, first, first_bias, second, second_bias)
    longer = (blocks[0].shape[0] + 3 * PACK, LANES)
    return pl.pallas_call(
        functools.partial(middle_kernel, group, groups, normalizer, pieces),
        in_specs=[whole(*a.shape) for a in operands],
        out_specs=[whole(*longer) for _ in blocks],
        out_shape=[jax.ShapeDtypeStruct(longer, BF16) for _ in blocks],
        scratch_shapes=[pltpu.VMEM(shape, BF16) for _ in range(4)]
        + [
            pltpu.VMEM(shape, F32),
            pltpu.VMEM((2, width + PACK, 2 * width), F32),
            pltpu.VMEM((pieces, 3 * PACK, LANES), BF16),
        ],
        compiler_params=limits(MIDDLE_MIB),
        cost_estimate=pl.CostEstimate(flops=7 * 10**9, bytes_accessed=4 * MIB, transcendentals=0),
    )(*operands)


def local_groups_of(array, groups):
    return lax.dynamic_slice_in_dim(array, lax.axis_index("blk") * groups, groups, axis=0)


def exchange(blocks):
    return lax.all_to_all(blocks, "lat", split_axis=0, concat_axis=0, tiled=True)


def pass_to(block, shift):
    count = lax.axis_size("lat")
    return lax.ppermute(block, "lat", [(place, place ^ shift) for place in range(count)])


def swap_blocks(blocks):
    return [pass_to(block, shift) if shift else block for block, shift in zip(blocks, slots(len(blocks)))]


def reduce_gradients(grads, lat_count):
    kinds, groups, width, twice = grads.shape
    piece = width * twice // lat_count
    split = grads.reshape(kinds * groups, lat_count, piece).transpose(1, 0, 2)
    if kinds * groups * piece % LANES == 0:
        split = split.reshape(lat_count, kinds * groups * piece // LANES, LANES)
    total = jnp.sum(exchange(split), axis=0)
    return total.reshape(kinds, groups, piece)


def with_kernels(field, cotangent, first_weight, first_bias, second_weight, second_bias):
    local_rows, col_count, channels = field.shape
    width = first_weight.shape[1]
    groups = channels // width
    lat_count = lax.axis_size("lat")
    row_count = local_rows * lat_count
    sub_count = KW // lat_count
    waves = zonal_waves(col_count, KW)
    table = (
        waves.reshape(col_count, 2, lat_count, sub_count).transpose(0, 2, 1, 3).reshape(col_count, 2 * KW)
    )
    factor = np.repeat(wave_factor(KW).reshape(lat_count, 1, sub_count), 2, axis=1)
    cosine, sines = meridian_waves(row_count)
    unit = np.eye(PACK, dtype=np.float32)
    mixer = np.concatenate(
        [np.kron(cosine.astype(np.float32), unit), np.kron(sines.astype(np.float32), unit)], axis=1
    ).astype(BF16)
    chunks = table.reshape(col_count, lat_count // 2, 2 * LANES).transpose(1, 0, 2)
    ahead, back = jnp.asarray(np.ascontiguousarray(chunks)), jnp.asarray(np.ascontiguousarray(table.T))
    wide_factor = jnp.asarray(factor.reshape(1, 2 * KW))
    tall_factor = jnp.asarray(factor.reshape(lat_count, 2 * sub_count))
    mixer = jnp.asarray(mixer)
    normalizer = 1.0 / math.sqrt(row_count * KW)
    mine = lax.axis_index("lat").astype(jnp.int32).reshape(1)
    field, cotangent = field.transpose(0, 2, 1), cotangent.transpose(0, 2, 1)

    arrived = [
        swap_blocks(zonal(mine, field, cotangent, ahead, wide_factor, group, width, lat_count))
        for group in range(groups)
    ]
    returned = [
        swap_blocks(
            middle(
                arrived[group], local_rows, mixer, first_weight, first_bias, second_weight, second_bias,
                group, groups, normalizer,
            )
        )
        for group in range(groups)
    ]
    results = []
    for group in range(groups):
        results = inverse(
            returned[group], back, tall_factor, field, cotangent, group, groups,
            2 * width * width // lat_count, results,
        )
    mixed, field_gradient = (result.transpose(0, 2, 1) for result in results[:2])
    return (mixed, field_gradient, results[2], results[3])


def gelu_value(values):
    tangent = jnp.tanh(GELU_SCALE * (values + GELU_CUBIC * values * values * values))
    return 0.5 * values * (1.0 + tangent)


def gelu_slope(values):
    tangent = jnp.tanh(GELU_SCALE * (values + GELU_CUBIC * values * values * values))
    inner = GELU_SCALE * (1.0 + 3.0 * GELU_CUBIC * values * values)
    return 0.5 * (1.0 + tangent) + 0.5 * values * (1.0 - tangent * tangent) * inner


def contract(pattern, former, latter):
    return jnp.einsum(pattern, former, latter, preferred_element_type=F32)


def complex_block(weights):
    width = weights.shape[1]
    real_part, imag_part = weights[:, :, :width], weights[:, :, width:]
    upper = jnp.stack([real_part, imag_part], axis=2)
    lower = jnp.stack([-imag_part, real_part], axis=2)
    return jnp.stack([upper, lower], axis=1)


def block_gradient(outer):
    real_part = outer[:, 0, :, 0, :] + outer[:, 1, :, 1, :]
    imag_part = outer[:, 0, :, 1, :] - outer[:, 1, :, 0, :]
    return jnp.concatenate([real_part, imag_part], axis=2)


def bias_layout(bias):
    groups, twice = bias.shape
    return bias.reshape(groups, 2, twice // 2).transpose(1, 0, 2)[None, :, None]


def plain(field, cotangent, first_weight, first_bias, second_weight, second_bias):
    local_rows, col_count, channels = field.shape
    width = first_weight.shape[1]
    groups = channels // width
    lat_count = lax.axis_size("lat")
    row_count = local_rows * lat_count
    ahead = jnp.asarray(zonal_waves(col_count, KW))
    factor = jnp.asarray(wave_factor(KW))
    cosine, sines = (jnp.asarray(t) for t in meridian_waves(row_count))
    forth = jnp.stack(
        [jnp.stack([cosine, sines], axis=-1), jnp.stack([-sines, cosine], axis=-1)], axis=1
    )
    first_block = complex_block(local_groups_of(first_weight, groups))
    second_block = complex_block(local_groups_of(second_weight, groups))

    def swap(array, split, concat):
        return lax.all_to_all(array, "lat", split_axis=split, concat_axis=concat, tiled=True)

    spectrum = contract("hwc,wrk->hrkc", field, ahead).astype(BF16)
    adjoint = (contract("hwc,wrk->hrkc", cotangent, ahead) * factor[:, None]).astype(BF16)
    modes, adjoint = swap(spectrum, 2, 0), swap(adjoint, 2, 0)
    block_shape = (row_count, 2, modes.shape[2], groups, width)
    inputs = contract("mphr,hrkc->mpkc", forth, modes).astype(BF16).reshape(block_shape)
    harmonic_adjoint = contract("mphr,hrkc->mpkc", forth, adjoint).reshape(block_shape)
    pre_first = contract("mrkgc,grcsd->mskgd", inputs, first_block) + bias_layout(
        local_groups_of(first_bias, groups)
    )
    hidden = gelu_value(pre_first).astype(BF16)
    pre_second = contract("mrkgc,grcsd->mskgd", hidden, second_block) + bias_layout(
        local_groups_of(second_bias, groups)
    )
    squashed = jnp.tanh(pre_second / SHRINK)
    shrunk = (pre_second - SHRINK * squashed).astype(BF16).reshape(modes.shape)
    second_adjoint = (harmonic_adjoint * (squashed * squashed)).astype(BF16)
    second_grad = block_gradient(contract("mrkgc,mskgd->grcsd", hidden, second_adjoint))
    hidden_adjoint = contract("mskgd,grcsd->mrkgc", second_adjoint, second_block)
    first_adjoint = (hidden_adjoint * gelu_slope(pre_first)).astype(BF16)
    first_grad = block_gradient(contract("mrkgc,mskgd->grcsd", inputs, first_adjoint))
    harmonics_adjoint = contract("mskgd,grcsd->mrkgc", first_adjoint, first_block).astype(BF16)
    synthesis = contract("mphr,mpkc->hrkc", forth, shrunk).astype(BF16)
    returned = contract(
        "mphr,mpkc->hrkc", forth, harmonics_adjoint.reshape(modes.shape)
    ).astype(BF16)
    mixed_modes, return_modes = swap(synthesis, 0, 2), swap(returned, 0, 2)
    gradients = reduce_gradients(
        jnp.stack([first_grad, second_grad]) * (1.0 / math.sqrt(row_count * KW)), lat_count
    )
    mixed_modes = (mixed_modes.astype(F32) * factor[:, None]).astype(BF16)
    mixed = (field.astype(F32) + contract("hrkc,wrk->hwc", mixed_modes, ahead)).astype(BF16)
    field_gradient = (
        cotangent.astype(F32) + contract("hrkc,wrk->hwc", return_modes, ahead)
    ).astype(BF16)
    return (mixed, field_gradient, gradients[0], gradients[1])


def on_device(field, *rest):
    local_rows, _, channels = field.shape
    lat_count = lax.axis_size("lat")
    fits = (
        KW == HALF * lat_count
        and channels == 2 * rest[1].shape[1]
        and local_rows * lat_count % 2 == 0
        and rest[1].shape[1] % (2 * PACK) == 0
        and local_rows * lat_count * PACK <= 512
        and lat_count & (lat_count - 1) == 0
        and rest[1].shape[1] % lat_count == 0
        and rest[1].shape[1] // lat_count <= PACK
        and 2 * rest[1].shape[1] == LANES + HALF
    )
    return (with_kernels if fits else plain)(field, *rest)


def solution(mesh):
    placed = (P(("rep", "lat"), None, "blk"), P(("rep", "lat"), None, "blk"), P(), P(), P(), P())
    return jax.shard_map(
        on_device,
        mesh=mesh,
        in_specs=placed,
        out_specs=(
            P(("rep", "lat"), None, "blk"),
            P(("rep", "lat"), None, "blk"),
            P(("rep", "blk"), "lat"),
            P(("rep", "blk"), "lat"),
        ),
        check_vma=False,
    )
```
